512 devices in a mesh: fsdp: 32 (over x, y), layer: 8 (over z), own: 2 (over core).
Axes of the slice: x: 4, y: 8, z: 8, core: 2. Of those that a mesh axis runs over, the one named last changes fastest.
Arguments:
- factor: bfloat16 [448, 512, 512], P('layer', ('fsdp', 'own')), as said below
- old_basis: bfloat16 [448, 512, 512], P('layer', ('fsdp', 'own')), as said below
- moment: bfloat16 [448, 1024, 512], P('layer', ('fsdp', 'own')), may hold values from -6 to 6
- owner_table: int32 [448, 1], P('layer'), may hold values from 0 to 63; in each aligned block of 56 rows (0 to 55, 56 to 111, ...) at most 2 rows name the same one
Outputs:
- moment_out: bfloat16 [448, 1024, 512], P('layer', ('fsdp', 'own'))
- owner_basis: bfloat16 [8, 128, 512, 512], P('layer', ('fsdp', 'own'))
The draws below stay inside these ranges and needn't reach their ends.
Inputs may be any that keep to these rules, and one draw needn't show every extreme that they name: `owner_table`: within each layer group's 56 blocks (the rows of one index of layer), no owner is named more than 2 times, a bound that some block reaches. `factor`: each block is symmetric with a dominant positive diagonal. `old_basis`: each block is the identity plus a dense perturbation, well conditioned but not orthonormal.
All inputs are finite; a program needn't handle non-finite values.
Results may differ from the reference program's by a relative error of at most 0.014.
Values may be sent and summed in bfloat16 or wider, within the bound.
A program may use at most 64 MiB of HBM per device.

```python
import math
import jax
import jax.numpy as jnp
import numpy as np
from jax import lax

BLOCK = 512
SLOTS = 2
OWNERS = 64
GROUP_BLOCKS = 56
GROUPS = 8
BLOCKS = 448
COLS = 1024


def draw_factor(key, part):
    key = jax.random.fold_in(key, 5)
    diag_key, jitter_key = jax.random.split(key)
    diagonal = jax.random.uniform(diag_key, (BLOCKS, BLOCK), jnp.float32, 3.0, 6.0)
    jitter = jax.random.normal(jitter_key, (BLOCKS, BLOCK, BLOCK), jnp.float32) * 0.032
    symmetric = jitter + jnp.swapaxes(jitter, 1, 2)
    identity = jnp.eye(BLOCK, dtype=jnp.float32)
    return (symmetric + identity[None] * diagonal[:, None, :]).astype(jnp.bfloat16)


def draw_old_basis(key, part):
    key = jax.random.fold_in(key, 9)
    jitter = jax.random.normal(key, (BLOCKS, BLOCK, BLOCK), jnp.float32)
    identity = jnp.eye(BLOCK, dtype=jnp.float32)
    return (identity[None] + jitter * (0.3 / BLOCK ** 0.5)).astype(jnp.bfloat16)


def block_scale(key, shape, cuts, low, largest):
    loudness = 1.0
    for axis_at, blocks in cuts:
        heights = jax.random.uniform(jax.random.fold_in(jax.random.fold_in(key, 6), axis_at), (blocks,), jnp.float32, low / len(cuts), largest / len(cuts))
        loudness = loudness * jnp.repeat(jnp.exp(heights), shape[axis_at] // blocks).reshape((-1,) + (1,) * (len(shape) - 1 - axis_at))
    return loudness


def shared_out(key, own, number, rows, count, top, reach, skew):
    sequence = jax.random.permutation(key, count)
    packed, usual = load_shares(count, rows * top, reach, skew, True), load_shares(count, rows * top, reach, skew, False)
    places = jnp.arange(count)

    def named(tallies, offset_by):
        used = int((tallies > 0).sum())
        fixed = max(1, used // 4)
        shifted = fixed + (places - fixed + offset_by * (used - fixed)) % max(1, count - fixed)
        return jnp.zeros((count,), jnp.int32).at[sequence[jnp.where(places < fixed, places, shifted)]].set(jnp.asarray(tallies, jnp.int32))

    tallies = jnp.where(number % 4 == 0, named(packed, number // 4), named(usual, number - number // 4 - 1))
    mixed = jax.random.permutation(jax.random.fold_in(own, 3), count)
    giver, sink = mixed[0:count // 2 * 2:2], mixed[1:count // 2 * 2:2]
    slack = jnp.minimum(tallies[giver] - 1, reach - tallies[sink]) // 2
    slack = jnp.where((giver == sequence[0]) | (sink == sequence[0]) | (tallies[sink] == 0), 0, jnp.maximum(slack, 0))
    shifted = jax.random.randint(jax.random.fold_in(own, 4), (count // 2,), 0, 1 << 20) % (slack + 1)
    tallies = tallies.at[giver].add(-shifted).at[sink].add(shifted)
    members = jnp.searchsorted(jnp.cumsum(tallies), jnp.arange(rows * top), side="right").astype(jnp.int32)
    listing = members.reshape(top, rows).T
    listing = listing[jax.random.permutation(jax.random.fold_in(own, 1), rows)]
    offset_by = jax.random.randint(jax.random.fold_in(own, 2), (rows, 1), 0, top)
    return jnp.take_along_axis(listing, (jnp.arange(top)[None, :] + offset_by) % top, axis=1)


def load_shares(amount, total, reach, slope, full):
    weights = [(1 << 20) // math.isqrt(grade ** slope) + 1 for grade in range(1, amount + 1)]
    largest = reach if full else min(reach, max(-(-total // amount), total * weights[0] // sum(weights)))
    least = 1 if total - largest >= amount - 1 else 0
    given, surplus = [largest] + [least] * (amount - 1), total - largest - least * (amount - 1)
    while surplus > 0:
        candidates = [i for i in range(1, amount) if given[i] < largest] or [i for i in range(1, amount) if given[i] < reach]
        whole, budget = sum([weights[i] for i in candidates]), surplus
        for i in candidates:
            extra = min(reach - given[i], max(1, budget * weights[i] // whole), surplus)
            given[i] = given[i] + extra
            surplus = surplus - extra
    return np.array(given)


def normal_values(key, dims, scale, most, shards=(), kind=jnp.bfloat16):
    drawn = jax.random.normal(key, dims, jnp.float32) * scale
    if len(shards) > 0:
        drawn = block_scale(key, dims, shards, -0.22, 0.18) * drawn
    return jnp.clip(drawn, min=-most, max=most).astype(kind)


def setup_inputs(seed: int = 0) -> dict:
    key_of = jax.random.split(jax.random.key(seed), 5)
    factor = draw_factor(jax.random.fold_in(key_of[4], 71), 0)
    old_basis = draw_old_basis(jax.random.fold_in(key_of[4], 71), 0)
    moment = normal_values(key_of[2], (BLOCKS, COLS, BLOCK), 1.0, 6.0, ((0, 8), (1, 64)))
    owner_table_keys = jax.random.split(jax.random.fold_in(key_of[3], 1), BLOCKS // GROUP_BLOCKS)
    owner_table_turns = jax.random.permutation(jax.random.fold_in(key_of[3], 3), BLOCKS // GROUP_BLOCKS)
    owner_table = jax.vmap(lambda own, number: shared_out(jax.random.fold_in(key_of[3], 2), own, number, GROUP_BLOCKS, OWNERS, 1, SLOTS, 2))(owner_table_keys, owner_table_turns).reshape((BLOCKS, 1))
    return dict(factor=factor, old_basis=old_basis, moment=moment, owner_table=owner_table)


def refresh_group(operands):
    factor, old_basis, moment, owners = operands
    power = jnp.einsum('bij,bjk->bik', factor.astype(jnp.float32), old_basis.astype(jnp.float32)).astype(jnp.bfloat16)
    power_wide = power.astype(jnp.float32)
    gram_matrix = jnp.einsum('bji,bjk->bik', power_wide, power_wide)
    lower_factor = jnp.linalg.cholesky(gram_matrix)
    fresh_basis = lax.linalg.triangular_solve(lower_factor, power_wide, left_side=False, lower=True, transpose_a=True).astype(jnp.bfloat16)
    rotation = jnp.einsum('bji,bjk->bik', old_basis.astype(jnp.float32), fresh_basis.astype(jnp.float32)).astype(jnp.bfloat16)
    rotated = jnp.einsum('bcj,bjk->bck', moment.astype(jnp.float32), rotation.astype(jnp.float32)).astype(jnp.bfloat16)
    position = jnp.arange(GROUP_BLOCKS).astype(jnp.int32)
    earlier = (owners[None, :] == owners[:, None]) & (position[None, :] < position[:, None])
    slot_rank = jnp.sum(earlier.astype(jnp.int32), axis=1).astype(jnp.int32)
    target = (owners * SLOTS + slot_rank).astype(jnp.int32)
    placed = jnp.zeros((OWNERS * SLOTS, BLOCK, BLOCK), jnp.bfloat16).at[target].set(fresh_basis)
    return (rotated, placed)

def reference(factor, old_basis, moment, owner_table):
    grouped = (factor.reshape(GROUPS, GROUP_BLOCKS, BLOCK, BLOCK), old_basis.reshape(GROUPS, GROUP_BLOCKS, BLOCK, BLOCK), moment.reshape(GROUPS, GROUP_BLOCKS, COLS, BLOCK), owner_table.reshape(GROUPS, GROUP_BLOCKS).astype(jnp.int32))
    rotated, placed = lax.map(refresh_group, grouped)
    return (rotated.reshape(BLOCKS, COLS, BLOCK), placed)
```

```python
import functools

import jax
import jax.numpy as jnp
from jax import lax
from jax.experimental import pallas as pl
from jax.experimental.pallas import tpu as pltpu
from jax.sharding import PartitionSpec as P

SLOTS = 2
HI = lax.Precision.HIGHEST
SUB = 32


def rows_of(v, s):
    return jnp.broadcast_to(v[s:s + 1, :], (8, 128))


def factor_sub(wide, aug, at):
    tiles = SUB // 8
    wide, aug = list(wide), list(aug)
    sub = lax.broadcasted_iota(jnp.int32, (8, 128), 0)
    cols = {}
    for q in range(SUB):
        for t in range(q // 8, tiles):
            cols[q, t] = jnp.broadcast_to(wide[t][:, at + q:at + q + 1], (8, 128))
    diag = [None] * tiles
    mix = [None] * tiles
    for j in range(0, SUB, 2):
        tj, sj = j // 8, j % 8
        a = rows_of(cols[j, tj], sj)
        b = rows_of(cols[j, tj], sj + 1)
        d = rows_of(cols[j + 1, tj], sj + 1)
        det = a * d - b * b
        r = 1.0 / det
        m0, m1 = {}, {}
        for t in range(tj, tiles):
            c0, c1 = cols[j, t], cols[j + 1, t]
            x0 = (c0 * d - c1 * b) * r
            x1 = (c1 * a - c0 * b) * r
            if t == tj:
                x0 = jnp.where(sub > sj + 1, x0, 0.0)
                x1 = jnp.where(sub > sj + 1, x1, 0.0)
            m0[t], m1[t] = x0, x1
        for q in range(j + 2, SUB):
            p0 = rows_of(cols[j, q // 8], q % 8)
            p1 = rows_of(cols[j + 1, q // 8], q % 8)
            for t in range(q // 8, tiles):
                cols[q, t] = cols[q, t] - m0[t] * p0 - m1[t] * p1
        w0, w1 = rows_of(wide[tj], sj), rows_of(wide[tj], sj + 1)
        x0, x1 = rows_of(aug[tj], sj), rows_of(aug[tj], sj + 1)
        for t in range(tj, tiles):
            wide[t] = wide[t] - m0[t] * w0 - m1[t] * w1
            aug[t] = aug[t] - m0[t] * x0 - m1[t] * x1
        ia = 1.0 / a
        e = det * ia
        mu = b * ia
        if sj == 0:
            diag[tj] = jnp.where(sub == 0, a, e)
            mix[tj] = jnp.where(sub == 1, mu, 0.0)
        else:
            diag[tj] = jnp.where(sub == sj, a, jnp.where(sub == sj + 1, e, diag[tj]))
            mix[tj] = jnp.where(sub == sj + 1, mu, mix[tj])
    for t in range(tiles):
        s = lax.rsqrt(diag[t])
        wide[t] = s * (wide[t] - mix[t] * pltpu.roll(wide[t], 1, 0))
        aug[t] = s * (aug[t] - mix[t] * pltpu.roll(aug[t], 1, 0))
    return wide, aug


def dot_t(a, b, prec=HI):
    return lax.dot_general(a, b, (((0,), (0,)), ((), ())), precision=prec, preferred_element_type=jnp.float32)


def factor_block(diags, augs):
    r = lax.broadcasted_iota(jnp.int32, (128, 128), 0)
    c = lax.broadcasted_iota(jnp.int32, (128, 128), 1)
    for x in augs:
        x[...] = (r == c).astype(jnp.float32)
    for i in range(128 // SUB):
        for s, x in zip(diags, augs):
            at = SUB * i
            wide = [s[at + 8 * t:at + 8 * t + 8, :] for t in range(SUB // 8)]
            aug = [x[at + 8 * t:at + 8 * t + 8, :] for t in range(SUB // 8)]
            wide, aug = factor_sub(wide, aug, at)
            for t in range(SUB // 8):
                x[at + 8 * t:at + 8 * t + 8, :] = aug[t]
            if i < 128 // SUB - 1:
                u = jnp.concatenate(wide, axis=0)
                rhs = jnp.concatenate([u, jnp.concatenate(aug, axis=0)], axis=1)
                upd = dot_t(u, rhs)
                nx = at + SUB
                s[nx:, :] = s[nx:, :] - upd[nx:, :128]
                x[nx:, :] = x[nx:, :] - upd[nx:, 128:]


def refresh_kernel(n, f_ref, b_ref, fresh_ref, rot_ref, *scr):
    m, d, x = scr[:n], scr[n:2 * n], scr[2 * n:3 * n]
    vacant = []
    for s in range(n):
        pt = lax.dot_general(
            b_ref[s], f_ref[s], (((0,), (1,)), ((), ())), preferred_element_type=jnp.float32
        ).astype(jnp.bfloat16)
        gram = lax.dot_general(
            pt, pt, (((1,), (1,)), ((), ())), preferred_element_type=jnp.float32
        )
        r = lax.broadcasted_iota(jnp.int32, (512, 512), 0)
        c = lax.broadcasted_iota(jnp.int32, (512, 512), 1)
        eye = (r == c).astype(jnp.float32)
        trace = jnp.sum(gram * eye, keepdims=True)
        m[s][:, :512] = gram + eye * (trace == 0.0).astype(jnp.float32)
        m[s][:, 512:] = pt.astype(jnp.float32)

    def outer(k, _):
        at = pl.multiple_of(k * 128, 128)
        for s in range(n):
            d[s][...] = m[s][pl.ds(at, 128), pl.ds(at, 128)]
        factor_block(d, x)
        for s in range(n):
            m[s][pl.ds(at, 128), :] = jnp.dot(
                x[s][...], m[s][pl.ds(at, 128), :], precision=HI, preferred_element_type=jnp.float32
            )
        for kk in range(3):

            @pl.when(k == kk)
            def _():
                for s in range(n):
                    lo = 128 * (kk + 1)
                    u = m[s][lo - 128:lo, lo:512]
                    m[s][lo:, lo:] = m[s][lo:, lo:] - dot_t(u, m[s][lo - 128:lo, lo:])

        return 0

    lax.fori_loop(0, 4, outer, 0)
    for s in range(n):
        ft = m[s][:, 512:]
        fresh_ref[s] = ft.T.astype(jnp.bfloat16)
        rot_ref[s] = lax.dot_general(
            b_ref[s],
            ft.astype(jnp.bfloat16),
            (((0,), (1,)), ((), ())),
            preferred_element_type=jnp.float32,
        ).astype(jnp.bfloat16)


def refresh(factor_slots, basis_slots, moment_slots):
    n, order, _ = factor_slots.shape
    out = jax.ShapeDtypeStruct((n, order, order), jnp.bfloat16)
    fresh, rotation = pl.pallas_call(
        functools.partial(refresh_kernel, n),
        out_shape=(out, out),
        scratch_shapes=[pltpu.VMEM((order, 2 * order), jnp.float32)] * n
        + [pltpu.VMEM((128, 128), jnp.float32)] * (2 * n),
        compiler_params=pltpu.CompilerParams(vmem_limit_bytes=40 * 2**20),
        cost_estimate=pl.CostEstimate(flops=5 * 10**9, bytes_accessed=4 * 2**20, transcendentals=0),
    )(factor_slots, basis_slots)
    rotated = jnp.einsum(
        "bcj,bjk->bck", moment_slots, rotation, preferred_element_type=jnp.float32
    ).astype(jnp.bfloat16)
    return (fresh, rotated)


def pack(selector, pieces, slot_count):
    share_count = selector.shape[0] // slot_count
    flat = jnp.dot(
        selector, pieces.reshape(pieces.shape[0], -1), preferred_element_type=jnp.float32
    ).astype(jnp.bfloat16)
    return flat.reshape(slot_count, share_count, pieces.shape[1], pieces.shape[2])


def deliver(first, second, third):
    return (
        lax.all_to_all(first, ("fsdp", "own"), split_axis=1, concat_axis=1, tiled=True),
        lax.all_to_all(second, ("fsdp", "own"), split_axis=1, concat_axis=1, tiled=True),
        lax.all_to_all(third, ("fsdp", "own"), split_axis=1, concat_axis=1, tiled=True),
    )


def per_device(factor, old_basis, moment, owner_table):
    shares = lax.axis_size(("fsdp", "own"))
    blocks, row_count, block_order = factor.shape
    col_count = moment.shape[1]
    owners = owner_table[:, 0]
    position = jnp.arange(blocks, dtype=jnp.int32)
    earlier = (owners[None, :] == owners[:, None]) & (position[None, :] < position[:, None])
    slot_rank = jnp.sum(earlier.astype(jnp.int32), axis=1)
    target = slot_rank * shares + owners
    picker = (jnp.arange(SLOTS * shares, dtype=jnp.int32)[:, None] == target[None, :]).astype(
        jnp.bfloat16
    )
    delivered = deliver(
        pack(picker, factor, SLOTS), pack(picker, old_basis, SLOTS), pack(picker, moment, SLOTS)
    )
    fresh_basis, rotated = refresh(
        delivered[0].reshape(SLOTS, block_order, block_order),
        delivered[1].reshape(SLOTS, block_order, block_order),
        delivered[2].reshape(SLOTS, shares * col_count, block_order),
    )
    returned = lax.all_to_all(
        rotated.reshape(SLOTS, shares, col_count, block_order),
        ("fsdp", "own"),
        split_axis=1,
        concat_axis=1,
        tiled=True,
    )
    gathered = jnp.einsum(
        "kb,kx->bx",
        picker,
        returned.reshape(SLOTS * shares, -1),
        preferred_element_type=jnp.float32,
    )
    moment_out = gathered.astype(jnp.bfloat16).reshape(blocks, col_count, block_order)
    owner_basis = fresh_basis[None]
    return (moment_out, owner_basis)


def solution(mesh):
    in_specs = (
        P("layer", ("fsdp", "own"), None),
        P("layer", ("fsdp", "own"), None),
        P("layer", ("fsdp", "own"), None),
        P("layer", None),
    )
    out_specs = (P("layer", ("fsdp", "own"), None), P("layer", ("fsdp", "own"), None, None))
    return jax.shard_map(
        per_device, mesh=mesh, in_specs=in_specs, out_specs=out_specs, check_vma=False
    )
```

```python
import functools

import jax
import jax.numpy as jnp
from jax import lax
from jax.experimental import pallas as pl
from jax.experimental.pallas import tpu as pltpu
from jax.sharding import PartitionSpec as P

SLOTS = 2
SHARES = 64
BLOCKS = 56
MOVERS = 56
ORDER = 512
PANEL = 128
FULL = ORDER + 3 * PANEL
SHORT = ORDER + 2 * PANEL
HI = lax.Precision.HIGHEST
SUB = 32


def rows_of(v, s):
    return jnp.broadcast_to(v[s:s + 1, :], (8, 128))


def factor_sub(wide, aug, at):
    tiles = SUB // 8
    wide, aug = list(wide), list(aug)
    sub = lax.broadcasted_iota(jnp.int32, (8, 128), 0)
    cols = {}
    for q in range(SUB):
        for t in range(q // 8, tiles):
            cols[q, t] = jnp.broadcast_to(wide[t][:, at + q:at + q + 1], (8, 128))
    diag = [None] * tiles
    mix = [None] * tiles
    for j in range(0, SUB, 2):
        tj, sj = j // 8, j % 8
        a = rows_of(cols[j, tj], sj)
        b = rows_of(cols[j, tj], sj + 1)
        d = rows_of(cols[j + 1, tj], sj + 1)
        det = a * d - b * b
        r = 1.0 / det
        m0, m1 = {}, {}
        for t in range(tj, tiles):
            c0, c1 = cols[j, t], cols[j + 1, t]
            x0 = (c0 * d - c1 * b) * r
            x1 = (c1 * a - c0 * b) * r
            if t == tj:
                x0 = jnp.where(sub > sj + 1, x0, 0.0)
                x1 = jnp.where(sub > sj + 1, x1, 0.0)
            m0[t], m1[t] = x0, x1
        for q in range(j + 2, SUB):
            p0 = rows_of(cols[j, q // 8], q % 8)
            p1 = rows_of(cols[j + 1, q // 8], q % 8)
            for t in range(q // 8, tiles):
                cols[q, t] = cols[q, t] - m0[t] * p0 - m1[t] * p1
        w0, w1 = rows_of(wide[tj], sj), rows_of(wide[tj], sj + 1)
        x0, x1 = rows_of(aug[tj], sj), rows_of(aug[tj], sj + 1)
        for t in range(tj, tiles):
            wide[t] = wide[t] - m0[t] * w0 - m1[t] * w1
            aug[t] = aug[t] - m0[t] * x0 - m1[t] * x1
        ia = 1.0 / a
        e = det * ia
        mu = b * ia
        if sj == 0:
            diag[tj] = jnp.where(sub == 0, a, e)
            mix[tj] = jnp.where(sub == 1, mu, 0.0)
        else:
            diag[tj] = jnp.where(sub == sj, a, jnp.where(sub == sj + 1, e, diag[tj]))
            mix[tj] = jnp.where(sub == sj + 1, mu, mix[tj])
    for t in range(tiles):
        s = lax.rsqrt(diag[t])
        wide[t] = s * (wide[t] - mix[t] * pltpu.roll(wide[t], 1, 0))
        aug[t] = s * (aug[t] - mix[t] * pltpu.roll(aug[t], 1, 0))
    return wide, aug


def dot_t(a, b, prec=HI):
    return lax.dot_general(a, b, (((0,), (0,)), ((), ())), precision=prec, preferred_element_type=jnp.float32)


def factor_block(diags, augs):
    r = lax.broadcasted_iota(jnp.int32, (128, 128), 0)
    c = lax.broadcasted_iota(jnp.int32, (128, 128), 1)
    for x in augs:
        x[...] = (r == c).astype(jnp.float32)
    for i in range(128 // SUB):
        for s, x in zip(diags, augs):
            at = SUB * i
            wide = [s[at + 8 * t:at + 8 * t + 8, :] for t in range(SUB // 8)]
            aug = [x[at + 8 * t:at + 8 * t + 8, :] for t in range(SUB // 8)]
            wide, aug = factor_sub(wide, aug, at)
            for t in range(SUB // 8):
                x[at + 8 * t:at + 8 * t + 8, :] = aug[t]
            if i < 128 // SUB - 1:
                u = jnp.concatenate(wide, axis=0)
                rhs = jnp.concatenate([u, jnp.concatenate(aug, axis=0)], axis=1)
                upd = dot_t(u, rhs)
                nx = at + SUB
                s[nx:, :] = s[nx:, :] - upd[nx:, :128]
                x[nx:, :] = x[nx:, :] - upd[nx:, 128:]


def at_share(t):
    return {"fsdp": t // 2, "own": lax.rem(t, 2)}


def remote(src, dst, send, recv, t):
    return pltpu.make_async_remote_copy(
        src_ref=src,
        dst_ref=dst,
        send_sem=send,
        recv_sem=recv,
        device_id=at_share(t),
        device_id_type=pl.DeviceIdType.MESH,
    )


def mover(d):
    return jnp.where(d < 48, d, 2 * d - 48)


def wide_f32(x):
    return x.astype(jnp.float32).reshape(-1, x.shape[-1])


def refresh_kernel(
    table,
    factor,
    basis,
    moment,
    moment_out,
    owner_basis,
    send0,
    send1,
    sendm,
    got0,
    got1,
    gotm,
    backs,
    backr,
    old,
    work,
    diag,
    inverse,
    rotation,
    sems,
    recv0,
    recv1,
    recvm,
    recvb,
):
    me = lax.axis_index("fsdp") * 2 + lax.axis_index("own")
    panel = me // 16
    long = panel < 2
    idle = (me >= 48) & (lax.rem(me, 2) == 1)
    moves = jnp.logical_not(idle)
    peer = lax.rem(me + 1, SHARES)

    barrier = pltpu.get_barrier_semaphore()

    def greet(k, _):
        pl.semaphore_signal(
            barrier,
            inc=1,
            device_id=at_share(lax.rem(me + k, SHARES)),
            device_id_type=pl.DeviceIdType.MESH,
        )
        return 0

    lax.fori_loop(1, SHARES, greet, 0)

    def pack(slot, send, t):
        b = table[slot * SHARES + t]
        send[t, :, :ORDER] = basis[b]
        for q in range(3):
            lane = pl.multiple_of(lax.rem(panel + q, 4) * PANEL, PANEL)
            send[t, :, ORDER + q * PANEL:ORDER + (q + 1) * PANEL] = factor[b, :, pl.ds(lane, PANEL)]

    def post(slot, send, got, recv, t):
        @pl.when(long)
        def _():
            remote(send.at[t], got.at[me], sems.at[slot], recv.at[0], t).start()

        @pl.when(jnp.logical_not(long))
        def _():
            remote(
                send.at[t, :, :SHORT], got.at[me, :, :SHORT], sems.at[slot], recv.at[1], t
            ).start()

    def arrive(got, recv):
        @pl.when(long)
        def _():
            remote(got.at[0:31], got.at[0:31], recv.at[0], recv.at[0], peer).wait_recv()
            part = got.at[0:32, :, :SHORT]
            remote(part, part, recv.at[1], recv.at[1], peer).wait_recv()

        @pl.when(jnp.logical_not(long))
        def _():
            remote(got.at[0:32], got.at[0:32], recv.at[0], recv.at[0], peer).wait_recv()
            part = got.at[0:31, :, :SHORT]
            remote(part, part, recv.at[1], recv.at[1], peer).wait_recv()

    def sent(slot, send):
        @pl.when(long)
        def _():
            remote(send.at[0:63], send.at[0:63], sems.at[slot], recv0.at[0], peer).wait_send()

        @pl.when(jnp.logical_not(long))
        def _():
            part = send.at[0:63, :, :SHORT]
            remote(part, part, sems.at[slot], recv0.at[0], peer).wait_send()

    def pack0(t, _):
        pack(0, send0, t)
        return 0

    lax.fori_loop(0, SHARES, pack0, 0)
    got0[me] = send0[me]
    pl.semaphore_wait(barrier, SHARES - 1)

    def post0(k, _):
        post(0, send0, got0, recv0, lax.rem(me + k, SHARES))
        return 0

    lax.fori_loop(1, SHARES, post0, 0)

    def pack1(t, _):
        pack(1, send1, t)
        sendm[t] = moment[table[t]]
        return 0

    lax.fori_loop(0, SHARES, pack1, 0)
    got1[me] = send1[me]
    gotm[me] = sendm[me]

    def load(got):
        whole = wide_f32(got[:, :, :ORDER]).astype(jnp.bfloat16)
        old[...] = whole
        part = {}
        for p in range(4):
            for q in range(3 if p < 2 else 2):
                lo = ORDER + q * PANEL
                x = wide_f32(got[16 * p:16 * p + 16, :, lo:lo + PANEL])
                part[p, (p + q) % 4] = x
                if q:
                    part[(p + q) % 4, p] = x.T
        full = jnp.concatenate(
            [jnp.concatenate([part[p, q] for q in range(4)], axis=1) for p in range(4)], axis=0
        ).astype(jnp.bfloat16)
        pt = lax.dot_general(
            whole, full, (((0,), (0,)), ((), ())), preferred_element_type=jnp.float32
        ).astype(jnp.bfloat16)
        work[:, :ORDER] = lax.dot_general(
            pt, pt, (((1,), (1,)), ((), ())), preferred_element_type=jnp.float32
        )
        work[:, ORDER:] = pt.astype(jnp.float32)

    def panel_step(k):
        at = pl.multiple_of(k * PANEL, PANEL)
        diag[...] = work[pl.ds(at, PANEL), pl.ds(at, PANEL)]
        factor_block([diag], [inverse])
        work[pl.ds(at, PANEL), :] = jnp.dot(
            inverse[...], work[pl.ds(at, PANEL), :], precision=HI, preferred_element_type=jnp.float32
        )
        for kk in range(3):

            @pl.when(k == kk)
            def _():
                lo = PANEL * (kk + 1)
                u = work[lo - PANEL:lo, lo:ORDER]
                work[lo:, lo:] = work[lo:, lo:] - dot_t(u, work[lo - PANEL:lo, lo:])

    def keep(slot):
        there = jnp.full((ORDER, ORDER), table[3 * SHARES + slot], jnp.int32)
        owner_basis[0, slot] = jnp.where(there > 0, work[:, ORDER:].T, 0.0).astype(jnp.bfloat16)

    def post1(k, _):
        post(1, send1, got1, recv1, lax.rem(me + k, SHARES))
        return 0

    def postm(k, _):
        t = mover(lax.rem(me + k, MOVERS))

        @pl.when(t != me)
        def _():
            remote(sendm.at[t], gotm.at[me], sems.at[2], recvm, t).start()

        return 0

    def rotate(i, _):
        cut = lax.rem(me // 8 + i, 8)
        rows = pl.ds(cut * 8, 8)
        x = gotm[rows].reshape(8 * 16, ORDER)
        y = jnp.dot(x, rotation[...], preferred_element_type=jnp.float32).astype(jnp.bfloat16)
        backs[rows] = y.reshape(8, 16, ORDER)

        def postb(k, _):
            t = cut * 8 + k

            @pl.when(t != me)
            def _():
                remote(backs.at[t], backr.at[me], sems.at[3], recvb, t).start()

            return 0

        lax.fori_loop(0, 8, postb, 0)
        return 0

    def step(i, _):
        @pl.when(i == 0)
        def _():
            arrive(got0, recv0)
            lax.fori_loop(1, SHARES, post1, 0)
            load(got0)

        @pl.when(i == 2)
        def _():
            lax.fori_loop(0, MOVERS, postm, 0)

        @pl.when(i == 4)
        def _():
            keep(0)
            rotation[...] = lax.dot_general(
                old[...],
                work[:, ORDER:].astype(jnp.bfloat16),
                (((0,), (1,)), ((), ())),
                preferred_element_type=jnp.float32,
            ).astype(jnp.bfloat16)
            arrive(got1, recv1)
            load(got1)

        @pl.when((i == 6) & moves)
        def _():
            remote(gotm.at[0:63], gotm.at[0:63], recvm, recvm, peer).wait_recv()
            lax.fori_loop(0, 8, rotate, 0)
            backr[me] = backs[me]

        panel_step(lax.rem(i, 4))
        return 0

    lax.fori_loop(0, 8, step, 0)
    keep(1)

    @pl.when(moves)
    def _():
        remote(backr.at[0:55], backr.at[0:55], recvb, recvb, peer).wait_recv()

    @pl.when(idle)
    def _():
        remote(backr.at[0:56], backr.at[0:56], recvb, recvb, peer).wait_recv()

    def place(b, _):
        moment_out[b] = backr[table[2 * SHARES + b]]
        return 0

    lax.fori_loop(0, BLOCKS, place, 0)

    sent(0, send0)
    sent(1, send1)

    @pl.when(moves)
    def _():
        remote(sendm.at[0:55], sendm.at[0:55], sems.at[2], recvm, peer).wait_send()
        remote(backs.at[0:63], backs.at[0:63], sems.at[3], recvb, peer).wait_send()

    @pl.when(idle)
    def _():
        remote(sendm.at[0:56], sendm.at[0:56], sems.at[2], recvm, peer).wait_send()


def plan(owners, me):
    blocks = jnp.arange(BLOCKS, dtype=jnp.int32)
    shares = jnp.arange(SHARES, dtype=jnp.int32)
    same = (owners[:, None] == owners[None, :]) & (blocks[None, :] < blocks[:, None])
    rank = jnp.sum(same.astype(jnp.int32), axis=1)
    idle = (shares >= 48) & (shares % 2 == 1)
    mine = owners[None, :] == shares[:, None]
    first = mine & (rank == 0)[None, :]
    second = mine & (rank == 1)[None, :]
    vacant = jnp.logical_not(jnp.any(mine, axis=1) | idle)
    guest = (rank == 1) | ((owners >= 48) & (owners % 2 == 1))
    vacant_at = jnp.sum(vacant[None, :] & (shares[None, :] < shares[:, None]), axis=1)
    guest_at = jnp.sum(guest[None, :] & (blocks[None, :] < blocks[:, None]), axis=1)
    hosted = vacant[:, None] & guest[None, :] & (vacant_at[:, None] == guest_at[None, :])
    slot0 = jnp.sum(jnp.where(first | hosted, blocks[None, :], 0), axis=1)
    slot1 = jnp.sum(jnp.where(second, blocks[None, :], 0), axis=1)
    moved = hosted | (first & jnp.logical_not(idle)[:, None])
    where = jnp.sum(jnp.where(moved, shares[:, None], 0), axis=0)
    keeps = jnp.stack([jnp.any(owners == me), jnp.any((owners == me) & (rank == 1))])
    return jnp.concatenate(
        [slot0, slot1, jnp.pad(where, (0, SHARES - BLOCKS)), jnp.pad(keeps.astype(jnp.int32), (0, SHARES - 2))]
    ).astype(jnp.int32)


def per_device(factor, old_basis, moment, owner_table):
    me = lax.axis_index("fsdp") * 2 + lax.axis_index("own")
    table = plan(owner_table[:, 0], me)
    bf16 = jnp.bfloat16
    vmem = pl.BlockSpec(memory_space=pltpu.VMEM)
    return pl.pallas_call(
        refresh_kernel,
        out_shape=(
            jax.ShapeDtypeStruct(moment.shape, bf16),
            jax.ShapeDtypeStruct((1, SLOTS, ORDER, ORDER), bf16),
        ),
        in_specs=[pl.BlockSpec(memory_space=pltpu.SMEM), vmem, vmem, vmem],
        out_specs=(vmem, vmem),
        scratch_shapes=[
            pltpu.VMEM((SHARES, 8, FULL), bf16),
            pltpu.VMEM((SHARES, 8, FULL), bf16),
            pltpu.VMEM((SHARES, 16, ORDER), bf16),
            pltpu.VMEM((SHARES, 8, FULL), bf16),
            pltpu.VMEM((SHARES, 8, FULL), bf16),
            pltpu.VMEM((SHARES, 16, ORDER), bf16),
            pltpu.VMEM((SHARES, 16, ORDER), bf16),
            pltpu.VMEM((SHARES, 16, ORDER), bf16),
            pltpu.VMEM((ORDER, ORDER), bf16),
            pltpu.VMEM((ORDER, 2 * ORDER), jnp.float32),
            pltpu.VMEM((PANEL, PANEL), jnp.float32),
            pltpu.VMEM((PANEL, PANEL), jnp.float32),
            pltpu.VMEM((ORDER, ORDER), bf16),
            pltpu.SemaphoreType.DMA((4,)),
            pltpu.SemaphoreType.DMA((2,)),
            pltpu.SemaphoreType.DMA((2,)),
            pltpu.SemaphoreType.DMA,
            pltpu.SemaphoreType.DMA,
        ],
        compiler_params=pltpu.CompilerParams(
            collective_id=0, has_side_effects=True, vmem_limit_bytes=48 * 2**20
        ),
        cost_estimate=pl.CostEstimate(flops=8 * 10**9, bytes_accessed=4 * 2**20, transcendentals=0),
    )(table, factor, old_basis, moment)


def solution(mesh):
    in_specs = (
        P("layer", ("fsdp", "own"), None),
        P("layer", ("fsdp", "own"), None),
        P("layer", ("fsdp", "own"), None),
        P("layer", None),
    )
    out_specs = (P("layer", ("fsdp", "own"), None), P("layer", ("fsdp", "own"), None, None))
    return jax.shard_map(
        per_device, mesh=mesh, in_specs=in_specs, out_specs=out_specs, check_vma=False
    )
```

```python
import functools

import jax
import jax.numpy as jnp
from jax import lax
from jax.experimental import pallas as pl
from jax.experimental.pallas import tpu as pltpu
from jax.sharding import PartitionSpec as P

SLOTS = 2
SHARES = 64
BLOCKS = 56
ORDER = 512
PANEL = 128
FULL = ORDER + 3 * PANEL
SHORT = ORDER + 2 * PANEL
HI = lax.Precision.HIGHEST
SUB = 32


def rows_of(v, s):
    return jnp.broadcast_to(v[s:s + 1, :], (8, 128))


def factor_sub(wide, aug, at):
    tiles = SUB // 8
    wide, aug = list(wide), list(aug)
    sub = lax.broadcasted_iota(jnp.int32, (8, 128), 0)
    cols = {}
    for q in range(SUB):
        for t in range(q // 8, tiles):
            cols[q, t] = jnp.broadcast_to(wide[t][:, at + q:at + q + 1], (8, 128))
    diag = [None] * tiles
    mix = [None] * tiles
    for j in range(0, SUB, 2):
        tj, sj = j // 8, j % 8
        a = rows_of(cols[j, tj], sj)
        b = rows_of(cols[j, tj], sj + 1)
        d = rows_of(cols[j + 1, tj], sj + 1)
        det = a * d - b * b
        r = 1.0 / det
        m0, m1 = {}, {}
        for t in range(tj, tiles):
            c0, c1 = cols[j, t], cols[j + 1, t]
            x0 = (c0 * d - c1 * b) * r
            x1 = (c1 * a - c0 * b) * r
            if t == tj:
                x0 = jnp.where(sub > sj + 1, x0, 0.0)
                x1 = jnp.where(sub > sj + 1, x1, 0.0)
            m0[t], m1[t] = x0, x1
        for q in range(j + 2, SUB):
            p0 = rows_of(cols[j, q // 8], q % 8)
            p1 = rows_of(cols[j + 1, q // 8], q % 8)
            for t in range(q // 8, tiles):
                cols[q, t] = cols[q, t] - m0[t] * p0 - m1[t] * p1
        w0, w1 = rows_of(wide[tj], sj), rows_of(wide[tj], sj + 1)
        x0, x1 = rows_of(aug[tj], sj), rows_of(aug[tj], sj + 1)
        for t in range(tj, tiles):
            wide[t] = wide[t] - m0[t] * w0 - m1[t] * w1
            aug[t] = aug[t] - m0[t] * x0 - m1[t] * x1
        ia = 1.0 / a
        e = det * ia
        mu = b * ia
        if sj == 0:
            diag[tj] = jnp.where(sub == 0, a, e)
            mix[tj] = jnp.where(sub == 1, mu, 0.0)
        else:
            diag[tj] = jnp.where(sub == sj, a, jnp.where(sub == sj + 1, e, diag[tj]))
            mix[tj] = jnp.where(sub == sj + 1, mu, mix[tj])
    for t in range(tiles):
        s = lax.rsqrt(diag[t])
        wide[t] = s * (wide[t] - mix[t] * pltpu.roll(wide[t], 1, 0))
        aug[t] = s * (aug[t] - mix[t] * pltpu.roll(aug[t], 1, 0))
    return wide, aug


def dot_t(a, b, prec=HI):
    return lax.dot_general(a, b, (((0,), (0,)), ((), ())), precision=prec, preferred_element_type=jnp.float32)


def factor_block(diags, augs):
    r = lax.broadcasted_iota(jnp.int32, (128, 128), 0)
    c = lax.broadcasted_iota(jnp.int32, (128, 128), 1)
    for x in augs:
        x[...] = (r == c).astype(jnp.float32)
    for i in range(128 // SUB):
        for s, x in zip(diags, augs):
            at = SUB * i
            wide = [s[at + 8 * t:at + 8 * t + 8, :] for t in range(SUB // 8)]
            aug = [x[at + 8 * t:at + 8 * t + 8, :] for t in range(SUB // 8)]
            wide, aug = factor_sub(wide, aug, at)
            for t in range(SUB // 8):
                x[at + 8 * t:at + 8 * t + 8, :] = aug[t]
            if i < 128 // SUB - 1:
                u = jnp.concatenate(wide, axis=0)
                rhs = jnp.concatenate([u, jnp.concatenate(aug, axis=0)], axis=1)
                upd = dot_t(u, rhs)
                nx = at + SUB
                s[nx:, :] = s[nx:, :] - upd[nx:, :128]
                x[nx:, :] = x[nx:, :] - upd[nx:, 128:]


def at_share(t):
    return {"fsdp": t // 2, "own": lax.rem(t, 2)}


def remote(src, dst, send, recv, t):
    return pltpu.make_async_remote_copy(
        src_ref=src,
        dst_ref=dst,
        send_sem=send,
        recv_sem=recv,
        device_id=at_share(t),
        device_id_type=pl.DeviceIdType.MESH,
    )


def is_idle(t):
    return (lax.rem(t, 2) == 1) & (lax.rem(t // 2, 4) == t // 16)


def wide_f32(x):
    return x.astype(jnp.float32).reshape(-1, x.shape[-1])


def refresh_kernel(
    owners,
    factor_hbm,
    basis_hbm,
    moment_hbm,
    moment_out,
    owner_basis,
    send0,
    send1,
    sendm,
    got0,
    got1,
    gotm,
    backs,
    backr,
    old,
    work,
    diag,
    inverse,
    rotation,
    factor,
    basis,
    moment,
    planned,
    table,
    sems,
    recv0,
    recv1,
    recvm,
    recvb,
    local,
):
    fetches = [
        pltpu.make_async_copy(src, dst, local.at[i])
        for i, (src, dst) in enumerate(
            ((basis_hbm, basis), (factor_hbm, factor), (moment_hbm, moment))
        )
    ]
    for fetch in fetches:
        fetch.start()
    me = lax.axis_index("fsdp") * 2 + lax.axis_index("own")
    panel = me // 16
    long = panel < 2
    idle = is_idle(me)
    moves = jnp.logical_not(idle)
    peer = lax.rem(me + 1, SHARES)

    barrier = pltpu.get_barrier_semaphore()

    def greet(k, _):
        pl.semaphore_signal(
            barrier,
            inc=1,
            device_id=at_share(lax.rem(me + k, SHARES)),
            device_id_type=pl.DeviceIdType.MESH,
        )
        return 0

    lax.fori_loop(1, SHARES, greet, 0)

    plan(owners, planned)
    tables = pltpu.make_async_copy(planned, table, local.at[3])
    tables.start()
    for fetch in fetches[:2]:
        fetch.wait()
    tables.wait()

    def pack(slot, send, t):
        b = table[slot, t]
        send[t, :, :ORDER] = basis[b]
        for q in range(3):
            lane = pl.multiple_of(lax.rem(panel + q, 4) * PANEL, PANEL)
            send[t, :, ORDER + q * PANEL:ORDER + (q + 1) * PANEL] = factor[b, :, pl.ds(lane, PANEL)]

    def post(slot, send, got, recv, t):
        @pl.when(long)
        def _():
            remote(send.at[t], got.at[me], sems.at[slot], recv.at[0], t).start()

        @pl.when(jnp.logical_not(long))
        def _():
            remote(
                send.at[t, :, :SHORT], got.at[me, :, :SHORT], sems.at[slot], recv.at[1], t
            ).start()

    def arrive(got, recv):
        @pl.when(long)
        def _():
            remote(got.at[0:31], got.at[0:31], recv.at[0], recv.at[0], peer).wait_recv()
            part = got.at[0:32, :, :SHORT]
            remote(part, part, recv.at[1], recv.at[1], peer).wait_recv()

        @pl.when(jnp.logical_not(long))
        def _():
            remote(got.at[0:32], got.at[0:32], recv.at[0], recv.at[0], peer).wait_recv()
            part = got.at[0:31, :, :SHORT]
            remote(part, part, recv.at[1], recv.at[1], peer).wait_recv()

    def sent(slot, send):
        @pl.when(long)
        def _():
            remote(send.at[0:63], send.at[0:63], sems.at[slot], recv0.at[0], peer).wait_send()

        @pl.when(jnp.logical_not(long))
        def _():
            part = send.at[0:63, :, :SHORT]
            remote(part, part, sems.at[slot], recv0.at[0], peer).wait_send()

    def pack0(t, _):
        pack(0, send0, t)
        return 0

    lax.fori_loop(0, SHARES, pack0, 0)
    got0[me] = send0[me]
    pl.semaphore_wait(barrier, SHARES - 1)

    def post0(k, _):
        post(0, send0, got0, recv0, lax.rem(me + k, SHARES))
        return 0

    lax.fori_loop(1, SHARES, post0, 0)

    fetches[2].wait()

    def packm(t, _):
        sendm[t] = moment[table[0, t]]
        return 0

    lax.fori_loop(0, SHARES, packm, 0)
    gotm[me] = sendm[me]

    def postm(half):
        def body(k, _):
            t = lax.rem(16 * panel + 32 * half + lax.rem(lax.rem(me, 16) + k, 32), SHARES)

            @pl.when((t != me) & jnp.logical_not(is_idle(t)))
            def _():
                remote(sendm.at[t], gotm.at[me], sems.at[2], recvm.at[half], t).start()

            return 0

        lax.fori_loop(0, 32, body, 0)

    postm(0)

    def pack1(t, _):
        pack(1, send1, t)
        return 0

    lax.fori_loop(0, SHARES, pack1, 0)
    got1[me] = send1[me]

    def load(got):
        whole = wide_f32(got[:, :, :ORDER]).astype(jnp.bfloat16)
        old[...] = whole
        part = {}
        for p in range(4):
            for q in range(3 if p < 2 else 2):
                lo = ORDER + q * PANEL
                x = wide_f32(got[16 * p:16 * p + 16, :, lo:lo + PANEL])
                part[p, (p + q) % 4] = x
                if q:
                    part[(p + q) % 4, p] = x.T
        full = jnp.concatenate(
            [jnp.concatenate([part[p, q] for q in range(4)], axis=1) for p in range(4)], axis=0
        ).astype(jnp.bfloat16)
        pt = lax.dot_general(
            whole, full, (((0,), (0,)), ((), ())), preferred_element_type=jnp.float32
        ).astype(jnp.bfloat16)
        work[:, :ORDER] = lax.dot_general(
            pt, pt, (((1,), (1,)), ((), ())), preferred_element_type=jnp.float32
        )
        work[:, ORDER:] = pt.astype(jnp.float32)

    def panel_step(k):
        at = pl.multiple_of(k * PANEL, PANEL)
        diag[...] = work[pl.ds(at, PANEL), pl.ds(at, PANEL)]
        factor_block([diag], [inverse])
        work[pl.ds(at, PANEL), :] = jnp.dot(
            inverse[...], work[pl.ds(at, PANEL), :], precision=HI, preferred_element_type=jnp.float32
        )
        for kk in range(3):

            @pl.when(k == kk)
            def _():
                lo = PANEL * (kk + 1)
                u = work[lo - PANEL:lo, lo:ORDER]
                work[lo:, lo:] = work[lo:, lo:] - dot_t(u, work[lo - PANEL:lo, lo:])

    def keep(slot):
        there = jnp.full((ORDER, ORDER), table[3 + slot, me], jnp.int32)
        owner_basis[0, slot] = jnp.where(there > 0, work[:, ORDER:].T, 0.0).astype(jnp.bfloat16)

    def post1(k, _):
        post(1, send1, got1, recv1, lax.rem(me + k, SHARES))
        return 0

    def rotate(i, _):
        cut = lax.rem(2 * panel + 6 + i, 8)
        rows = pl.ds(cut * 8, 8)
        x = gotm[rows].reshape(8 * 16, ORDER)
        y = jnp.dot(x, rotation[...], preferred_element_type=jnp.float32).astype(jnp.bfloat16)
        backs[rows] = y.reshape(8, 16, ORDER)

        def postb(k, _):
            t = cut * 8 + k

            @pl.when(t != me)
            def _():
                remote(backs.at[t], backr.at[me], sems.at[3], recvb, t).start()

            return 0

        lax.fori_loop(0, 8, postb, 0)
        return 0

    def step(i, _):
        @pl.when(i == 0)
        def _():
            arrive(got0, recv0)
            lax.fori_loop(1, SHARES, post1, 0)
            load(got0)

        @pl.when(i == 2)
        def _():
            postm(1)

        @pl.when(i == 4)
        def _():
            keep(0)
            rotation[...] = lax.dot_general(
                old[...],
                work[:, ORDER:].astype(jnp.bfloat16),
                (((0,), (1,)), ((), ())),
                preferred_element_type=jnp.float32,
            ).astype(jnp.bfloat16)

            @pl.when(moves)
            def _():
                remote(gotm.at[0:31], gotm.at[0:31], sems.at[2], recvm.at[0], peer).wait_recv()
                lax.fori_loop(0, 4, rotate, 0)
                backr[me] = backs[me]

            arrive(got1, recv1)
            load(got1)

        @pl.when((i == 6) & moves)
        def _():
            remote(gotm.at[0:32], gotm.at[0:32], sems.at[2], recvm.at[1], peer).wait_recv()
            lax.fori_loop(4, 8, rotate, 0)

        panel_step(lax.rem(i, 4))
        return 0

    lax.fori_loop(0, 8, step, 0)
    keep(1)

    @pl.when(moves)
    def _():
        remote(backr.at[0:55], backr.at[0:55], recvb, recvb, peer).wait_recv()

    @pl.when(idle)
    def _():
        remote(backr.at[0:56], backr.at[0:56], recvb, recvb, peer).wait_recv()

    def place(b, _):
        moment_out[b] = backr[table[2, b]]
        return 0

    lax.fori_loop(0, BLOCKS, place, 0)

    sent(0, send0)
    sent(1, send1)

    @pl.when(moves)
    def _():
        remote(sendm.at[0:55], sendm.at[0:55], sems.at[2], recvb, peer).wait_send()
        remote(backs.at[0:63], backs.at[0:63], sems.at[3], recvb, peer).wait_send()

    @pl.when(idle)
    def _():
        remote(sendm.at[0:56], sendm.at[0:56], sems.at[2], recvb, peer).wait_send()


def plan(owners, planned):
    shape = (PANEL, PANEL)
    sub = lax.broadcasted_iota(jnp.int32, shape, 0)
    lane = lax.broadcasted_iota(jnp.int32, shape, 1)
    column = jnp.broadcast_to(
        jnp.concatenate([owners[...], jnp.full((PANEL - BLOCKS, 1), -1, jnp.int32)], axis=0), shape
    )
    row = column.T

    def across(x):
        return jnp.broadcast_to(jnp.sum(x.astype(jnp.int32), axis=1, keepdims=True), shape)

    def down(x):
        return jnp.broadcast_to(jnp.sum(x.astype(jnp.int32), axis=0, keepdims=True), shape)

    def resting(t):
        return ((t & 1) == 1) & (((t >> 1) & 3) == (t >> 4))

    same = column == row
    rank_c = across(same & (lane < sub))
    rank_r = down(same & (sub < lane))
    mine = column == lane
    first = mine & (rank_c == 0)
    second = mine & (rank_c == 1)
    owned_r = down(mine)
    owned_c = across(row == sub)
    vacant_r = (owned_r == 0) & jnp.logical_not(resting(lane)) & (lane < SHARES)
    vacant_c = (owned_c == 0) & jnp.logical_not(resting(sub)) & (sub < SHARES)
    guest_c = (column >= 0) & ((rank_c == 1) | resting(column))
    guest_r = (row >= 0) & ((rank_r == 1) | resting(row))
    vacant_at = down(vacant_c & (sub < lane))
    guest_at = across(guest_r & (lane < sub))
    hosted = guest_c & vacant_r & (vacant_at == guest_at)
    zero = jnp.zeros(shape, jnp.int32)
    moved = hosted | (first & jnp.logical_not(resting(lane)))
    rows = (
        down(jnp.where(first | hosted, sub, zero)),
        down(jnp.where(second, sub, zero)),
        across(jnp.where(moved, lane, zero)).T,
        owned_r,
        down(second),
    )
    for i, x in enumerate(rows):
        planned[i:i + 1, :] = x[0:1, :]


def per_device(factor, old_basis, moment, owner_table):
    bf16 = jnp.bfloat16
    vmem = pl.BlockSpec(memory_space=pltpu.VMEM)
    hbm = pl.BlockSpec(memory_space=pl.ANY)
    return pl.pallas_call(
        refresh_kernel,
        out_shape=(
            jax.ShapeDtypeStruct(moment.shape, bf16),
            jax.ShapeDtypeStruct((1, SLOTS, ORDER, ORDER), bf16),
        ),
        in_specs=[vmem, hbm, hbm, hbm],
        out_specs=(vmem, vmem),
        scratch_shapes=[
            pltpu.VMEM((SHARES, 8, FULL), bf16),
            pltpu.VMEM((SHARES, 8, FULL), bf16),
            pltpu.VMEM((SHARES, 16, ORDER), bf16),
            pltpu.VMEM((SHARES, 8, FULL), bf16),
            pltpu.VMEM((SHARES, 8, FULL), bf16),
            pltpu.VMEM((SHARES, 16, ORDER), bf16),
            pltpu.VMEM((SHARES, 16, ORDER), bf16),
            pltpu.VMEM((SHARES, 16, ORDER), bf16),
            pltpu.VMEM((ORDER, ORDER), bf16),
            pltpu.VMEM((ORDER, 2 * ORDER), jnp.float32),
            pltpu.VMEM((PANEL, PANEL), jnp.float32),
            pltpu.VMEM((PANEL, PANEL), jnp.float32),
            pltpu.VMEM((ORDER, ORDER), bf16),
            pltpu.VMEM(factor.shape, bf16),
            pltpu.VMEM(old_basis.shape, bf16),
            pltpu.VMEM(moment.shape, bf16),
            pltpu.VMEM((8, PANEL), jnp.int32),
            pltpu.SMEM((8, PANEL), jnp.int32),
            pltpu.SemaphoreType.DMA((4,)),
            pltpu.SemaphoreType.DMA((2,)),
            pltpu.SemaphoreType.DMA((2,)),
            pltpu.SemaphoreType.DMA((2,)),
            pltpu.SemaphoreType.DMA,
            pltpu.SemaphoreType.DMA((4,)),
        ],
        compiler_params=pltpu.CompilerParams(
            collective_id=0, has_side_effects=True, vmem_limit_bytes=60 * 2**20
        ),
        cost_estimate=pl.CostEstimate(flops=8 * 10**9, bytes_accessed=4 * 2**20, transcendentals=0),
    )(owner_table, factor, old_basis, moment)


def solution(mesh):
    in_specs = (
        P("layer", ("fsdp", "own"), None),
        P("layer", ("fsdp", "own"), None),
        P("layer", ("fsdp", "own"), None),
        P("layer", None),
    )
    out_specs = (P("layer", ("fsdp", "own"), None), P("layer", ("fsdp", "own"), None, None))
    return jax.shard_map(
        per_device, mesh=mesh, in_specs=in_specs, out_specs=out_specs, check_vma=False
    )
```

```python
import functools

import jax
import jax.numpy as jnp
from jax import lax
from jax.experimental import pallas as pl
from jax.experimental.pallas import tpu as pltpu
from jax.sharding import PartitionSpec as P

SLOTS = 2
SHARES = 64
BLOCKS = 56
ORDER = 512
PANEL = 128
WIDTHS = ((ORDER + 3 * PANEL, ORDER + 2 * PANEL), (ORDER + 2 * PANEL, ORDER + PANEL))
SUB = 32


def rows_of(v, s):
    return jnp.broadcast_to(v[s:s + 1, :], (8, 128))


def split(x):
    high = x.astype(jnp.bfloat16)
    return high, (x - high.astype(jnp.float32)).astype(jnp.bfloat16)


def left(x, axis):
    high, low = split(x)
    return jnp.concatenate([high, high, low], axis=axis)


def right(x):
    high, low = split(x)
    return jnp.concatenate([high, low, high], axis=0)


def dot_of(a, b, axis):
    return lax.dot_general(a, b, (((axis,), (0,)), ((), ())), preferred_element_type=jnp.float32)


def inverse_of(x):
    r = pl.reciprocal(x, approx=True)
    return r * (2.0 - x * r)


def factor_sub(wide, aug, at):
    tiles = SUB // 8
    wide, aug = list(wide), list(aug)
    sub = lax.broadcasted_iota(jnp.int32, (8, 128), 0)
    cols = {}
    for q in range(SUB):
        for t in range(q // 8, tiles):
            cols[q, t] = jnp.broadcast_to(wide[t][:, at + q:at + q + 1], (8, 128))
    diag = [None] * tiles
    mix = [None] * tiles
    for j in range(0, SUB, 2):
        tj, sj = j // 8, j % 8
        a = rows_of(cols[j, tj], sj)
        b = rows_of(cols[j, tj], sj + 1)
        d = rows_of(cols[j + 1, tj], sj + 1)
        det = a * d - b * b
        r = inverse_of(det)
        m0, m1 = {}, {}
        for t in range(tj, tiles):
            c0, c1 = cols[j, t], cols[j + 1, t]
            x0 = c0 * d - c1 * b
            x1 = c1 * a - c0 * b
            if t == tj:
                x0 = jnp.where(sub > sj + 1, x0, 0.0)
                x1 = jnp.where(sub > sj + 1, x1, 0.0)
            m0[t], m1[t] = x0 * r, x1 * r
        for q in range(j + 2, SUB):
            p0 = rows_of(cols[j, q // 8], q % 8)
            p1 = rows_of(cols[j + 1, q // 8], q % 8)
            for t in range(q // 8, tiles):
                cols[q, t] = cols[q, t] - (m0[t] * p0 + m1[t] * p1)
        w0, w1 = rows_of(wide[tj], sj), rows_of(wide[tj], sj + 1)
        x0, x1 = rows_of(aug[tj], sj), rows_of(aug[tj], sj + 1)
        for t in range(tj, tiles):
            wide[t] = wide[t] - m0[t] * w0 - m1[t] * w1
            aug[t] = aug[t] - m0[t] * x0 - m1[t] * x1
        ia = inverse_of(a)
        e = det * ia
        mu = b * ia
        if sj == 0:
            diag[tj] = jnp.where(sub == 0, a, e)
            mix[tj] = jnp.where(sub == 1, mu, 0.0)
        else:
            diag[tj] = jnp.where(sub == sj, a, jnp.where(sub == sj + 1, e, diag[tj]))
            mix[tj] = jnp.where(sub == sj + 1, mu, mix[tj])
    for t in range(tiles):
        s = lax.rsqrt(diag[t])
        wide[t] = s * (wide[t] - mix[t] * pltpu.roll(wide[t], 1, 0))
        aug[t] = s * (aug[t] - mix[t] * pltpu.roll(aug[t], 1, 0))
    return wide, aug


def dot_t(a, b):
    return dot_of(left(a, 0), right(b), 0)


def factor_block(diags, augs):
    r = lax.broadcasted_iota(jnp.int32, (128, 128), 0)
    c = lax.broadcasted_iota(jnp.int32, (128, 128), 1)
    for x in augs:
        x[...] = (r == c).astype(jnp.float32)
    for i in range(128 // SUB):
        for s, x in zip(diags, augs):
            at = SUB * i
            wide = [s[at + 8 * t:at + 8 * t + 8, :] for t in range(SUB // 8)]
            aug = [x[at + 8 * t:at + 8 * t + 8, :] for t in range(SUB // 8)]
            wide, aug = factor_sub(wide, aug, at)
            for t in range(SUB // 8):
                x[at + 8 * t:at + 8 * t + 8, :] = aug[t]
            if i < 128 // SUB - 1:
                u = jnp.concatenate(wide, axis=0)
                both = right(jnp.concatenate([u, jnp.concatenate(aug, axis=0)], axis=1))
                turned = left(u, 0)
                nx = at + SUB
                upd = dot_of(turned[:, nx:], both, 0)
                s[nx:, :] = s[nx:, :] - upd[:, :128]
                x[nx:, :] = x[nx:, :] - upd[:, 128:]


def at_share(t):
    return {"fsdp": t // 2, "own": lax.rem(t, 2)}


def share(x, y, c):
    return x * 16 + lax.rem(y + 8, 8) * 2 + c


def remote(src, dst, send, recv, t):
    return pltpu.make_async_remote_copy(
        src_ref=src,
        dst_ref=dst,
        send_sem=send,
        recv_sem=recv,
        device_id=at_share(t),
        device_id_type=pl.DeviceIdType.MESH,
    )


def is_idle(t):
    return (lax.rem(t, 2) == 1) & (lax.rem(t // 2, 4) == t // 16)


def wide_f32(x):
    return x.astype(jnp.float32).reshape(-1, x.shape[-1])


def refresh_kernel(
    owners,
    factor_hbm,
    basis_hbm,
    moment_hbm,
    moment_out,
    owner_basis,
    send0,
    send1,
    sendm,
    got0,
    got1,
    gotm,
    backs,
    backr,
    old,
    work,
    diag,
    inverse,
    rots,
    factor,
    basis,
    moment,
    planned,
    table,
    sent,
    recv0,
    recv1,
    recvm,
    recvr,
    recvb,
    local,
):
    fetches = [
        pltpu.make_async_copy(src, dst, local.at[i])
        for i, (src, dst) in enumerate(
            ((basis_hbm, basis), (factor_hbm, factor), (moment_hbm, moment))
        )
    ]
    for fetch in fetches:
        fetch.start()

    me = lax.axis_index("fsdp") * 2 + lax.axis_index("own")
    panel = me // 16
    line = lax.rem(me // 2, 8)
    core = lax.rem(me, 2)
    seat = panel * 2 + core
    peer = lax.rem(me + 1, SHARES)
    hosts = (me, share(panel, line - 1, core), share(panel, line + 1, core))
    active = [jnp.logical_not(is_idle(t)) for t in hosts]
    few = active[0] & active[1] & active[2]
    short = ((panel < 2) & (core == 1), (panel >= 2) & (core == 0))

    barrier = pltpu.get_barrier_semaphore()

    def greet(k, _):
        pl.semaphore_signal(
            barrier,
            inc=1,
            device_id=at_share(lax.rem(me + k, SHARES)),
            device_id_type=pl.DeviceIdType.MESH,
        )
        return 0

    lax.fori_loop(1, SHARES, greet, 0)

    plan(owners, planned)
    tables = pltpu.make_async_copy(planned, table, local.at[3])
    tables.start()
    for fetch in fetches[:2]:
        fetch.wait()
    tables.wait()

    def piece(b, turn):
        lane = pl.multiple_of(lax.rem(panel + turn, 4) * PANEL, PANEL)
        return factor[b, :, pl.ds(lane, PANEL)]

    tile_lane = lax.broadcasted_iota(jnp.int32, (8, PANEL), 1)
    odd = ((tile_lane >> 3) & 1) == 1
    whole_diag = jnp.logical_not(odd) | (jnp.full((8, PANEL), core, jnp.int32) == 1)
    whole_far = odd | (jnp.full((8, PANEL), panel, jnp.int32) < 2)

    def merge(mask, mine, other, turn):
        turned = pltpu.roll(other.astype(jnp.float32), turn, 1)
        return jnp.where(mask, mine.astype(jnp.float32), turned).astype(jnp.bfloat16)

    def pack0(t):
        a, b = table[0, t], table[1, t]
        send0[t, :, :ORDER] = basis[a]
        send0[t, :, ORDER:ORDER + PANEL] = piece(a, 1)
        send0[t, :, ORDER + PANEL:ORDER + 2 * PANEL] = merge(whole_diag, piece(a, 0), piece(b, 0), 8)
        send0[t, :, ORDER + 2 * PANEL:] = merge(whole_far, piece(a, 2), piece(b, 2), PANEL - 8)

    def pack1(t):
        b = table[1, t]
        send1[t, :, :ORDER] = basis[b]
        send1[t, :, ORDER:ORDER + PANEL] = piece(b, 1)
        send1[t, :, ORDER + PANEL:] = piece(b, 2 * (1 - core))

    def post(slot, pack, send, got, recv):
        long_width, short_width = WIDTHS[slot]

        def body(k, _):
            t = lax.rem(me + k, SHARES)
            pack(t)

            @pl.when(jnp.logical_not(short[slot]))
            def _():
                remote(send.at[t], got.at[me], sent.at[slot], recv.at[0], t).start()

            @pl.when(short[slot])
            def _():
                remote(
                    send.at[t, :, :short_width],
                    got.at[me, :, :short_width],
                    sent.at[slot],
                    recv.at[1],
                    t,
                ).start()

            return 0

        lax.fori_loop(1, SHARES, body, 0)
        pack(me)
        got[me] = send[me]

    def arrive(slot, got, recv):
        long_width, short_width = WIDTHS[slot]

        def take(longs, shorts):
            part = got.at[0:longs]
            remote(part, part, recv.at[0], recv.at[0], peer).wait_recv()
            part = got.at[0:shorts, :, :short_width]
            remote(part, part, recv.at[1], recv.at[1], peer).wait_recv()

        @pl.when(jnp.logical_not(short[slot]))
        def _():
            take(47, 16)

        @pl.when(short[slot])
        def _():
            take(48, 15)

    def flush(slot, send):
        long_width, short_width = WIDTHS[slot]

        @pl.when(jnp.logical_not(short[slot]))
        def _():
            part = send.at[0:63]
            remote(part, part, sent.at[slot], recvb, peer).wait_send()

        @pl.when(short[slot])
        def _():
            part = send.at[0:63, :, :short_width]
            remote(part, part, sent.at[slot], recvb, peer).wait_send()

    def route(t):
        gap = lax.rem(line - lax.rem(t // 2, 8) + 8, 8)
        above = (gap > 0) & ((gap < 4) | ((gap == 4) & (core == 0)))
        region = jnp.where(gap == 0, 0, jnp.where(above, 1, 2))
        dest = share(t // 16, lax.rem(t // 2, 8) + jnp.where(region == 2, 7, region), lax.rem(t, 2))
        place = jnp.where(gap == 0, 0, jnp.where(above, gap, 12 - gap)) * 8 + seat
        return dest, region, place

    def postm(k, _):
        t = lax.rem(me + k, SHARES)
        sendm[t] = moment[table[0, t]]
        dest, region, place = route(t)

        @pl.when((dest != me) & jnp.logical_not(is_idle(t)))
        def _():
            remote(sendm.at[t], gotm.at[place], sent.at[2], recvm.at[region], dest).start()

        return 0

    def load(slot):
        got = (got0, got1)[slot]
        whole = wide_f32(got[:, :, :ORDER]).astype(jnp.bfloat16)
        old[...] = whole
        row_odd = ((lax.broadcasted_iota(jnp.int32, (PANEL, PANEL), 0) >> 3) & 1) == 1
        lane_odd = ((lax.broadcasted_iota(jnp.int32, (PANEL, PANEL), 1) >> 3) & 1) == 1

        def tile(ref, p, q):
            lo = ORDER + q * PANEL
            return wide_f32(ref[16 * p:16 * p + 16, :, lo:lo + PANEL])

        part = {}
        for p in range(4):
            q = (p + 1) % 4
            part[p, q] = tile(got, p, 0)
            part[q, p] = part[p, q].T
            own = tile(got0, p, 1)
            if slot == 1:
                own = jnp.where(row_odd, tile(got1, p, 1), pltpu.roll(own, PANEL - 8, 1))
            part[p, p] = jnp.where(row_odd | jnp.logical_not(lane_odd), own, own.T)
        for p in range(2):
            near, far = tile(got0, p, 2), tile(got0, p + 2, 2)
            if slot == 1:
                near, far = tile(got1, p, 1), pltpu.roll(far, 8, 1)
            part[p, p + 2] = jnp.where(row_odd, far.T, near)
            part[p + 2, p] = part[p, p + 2].T
        full = jnp.concatenate(
            [jnp.concatenate([part[p, q] for q in range(4)], axis=1) for p in range(4)], axis=0
        ).astype(jnp.bfloat16)
        pt = lax.dot_general(
            whole, full, (((0,), (0,)), ((), ())), preferred_element_type=jnp.float32
        ).astype(jnp.bfloat16)
        work[:, :ORDER] = lax.dot_general(
            pt, pt, (((1,), (1,)), ((), ())), preferred_element_type=jnp.float32
        )
        work[:, ORDER:] = pt.astype(jnp.float32)

    def panel_step(k):
        at = pl.multiple_of(k * PANEL, PANEL)
        diag[...] = work[pl.ds(at, PANEL), pl.ds(at, PANEL)]
        factor_block([diag], [inverse])
        work[pl.ds(at, PANEL), :] = dot_of(
            left(inverse[...], 1), right(work[pl.ds(at, PANEL), :]), 1
        )
        for kk in range(3):

            @pl.when(k == kk)
            def _():
                lo = PANEL * (kk + 1)
                u = work[lo - PANEL:lo, lo:ORDER]
                work[lo:, lo:] = work[lo:, lo:] - dot_t(u, work[lo - PANEL:lo, lo:])

    def keep(slot):
        there = jnp.full((ORDER, ORDER), table[3 + slot, me], jnp.int32)
        owner_basis[0, slot] = jnp.where(there > 0, work[:, ORDER:].T, 0.0).astype(jnp.bfloat16)

    def rotate(region, low, high):
        host = hosts[region]

        def group(g, _):
            rows = pl.ds(pl.multiple_of(g * 8, 8), 8)
            x = gotm[rows].reshape(8 * 16, ORDER)
            y = jnp.dot(x, rots[region], preferred_element_type=jnp.float32).astype(jnp.bfloat16)
            backs[rows] = y.reshape(8, 16, ORDER)
            away = g - low
            place = line + (away if region == 1 else -away)

            def reply(k, _):
                t = share(k // 2, place, lax.rem(k, 2))
                ours = jnp.logical_or(away < 3, lax.rem(k, 2) == region - 1)

                @pl.when((t != me) & ours)
                def _():
                    remote(
                        backs.at[g * 8 + k], backr.at[host], sent.at[3 + region], recvb, t
                    ).start()

                return 0

            lax.fori_loop(0, 8, reply, 0)
            return 0

        lax.fori_loop(low, high, group, 0)
        backr[host] = backs[low * 8 + seat]

    def took(region, wait_in):
        part = gotm.at[0:7] if region == 0 else gotm.at[0:27]
        if wait_in:
            remote(part, part, sent.at[2], recvm.at[region], peer).wait_recv()
        else:
            remote(part, part, sent.at[3 + region], recvb, peer).wait_send()

    def post_moments():
        lax.fori_loop(0, SHARES, postm, 0)
        for region in range(3):
            gotm[(0, 8, 40)[region] + seat] = sendm[hosts[region]]

    pl.semaphore_wait(barrier, SHARES - 1)
    post(0, pack0, send0, got0, recv0)
    post(1, pack1, send1, got1, recv1)
    fetches[2].wait()
    if 0 < 0:
        post_moments()

    def step(i, _):
        @pl.when(i == 0)
        def _():
            arrive(0, got0, recv0)
            if 0 == 0:
                post_moments()
            load(0)

        if 0 > 0:

            @pl.when(i == 0)
            def _():
                post_moments()

        @pl.when(i == 4)
        def _():
            keep(0)

            @pl.when(active[0])
            def _():
                rots[0] = lax.dot_general(
                    old[...],
                    work[:, ORDER:].astype(jnp.bfloat16),
                    (((0,), (1,)), ((), ())),
                    preferred_element_type=jnp.float32,
                ).astype(jnp.bfloat16)
                for q in range(4):
                    rows = pl.ds(q * PANEL, PANEL)
                    for side in range(2):
                        remote(
                            rots.at[0, rows],
                            rots.at[2 - side, rows],
                            sent.at[6],
                            recvr.at[1 - side],
                            hosts[1 + side],
                        ).start()

            arrive(1, got1, recv1)
            load(1)

        @pl.when((i == 5) & active[0])
        def _():
            took(0, True)
            rotate(0, 0, 1)

        for region in (1, 2):

            @pl.when((i == 6) & active[region])
            def _():
                took(region, True)
                remote(rots.at[0], rots.at[region], sent.at[6], recvr.at[region - 1], peer).wait_recv()
                rotate(region, 4 * region - 3, 4 * region + 1)

        panel_step(lax.rem(i, 4))
        return 0

    lax.fori_loop(0, 8, step, 0)
    keep(1)

    @pl.when(few)
    def _():
        remote(backr.at[0:53], backr.at[0:53], sent.at[2], recvb, peer).wait_recv()

    @pl.when(jnp.logical_not(few))
    def _():
        remote(backr.at[0:54], backr.at[0:54], sent.at[2], recvb, peer).wait_recv()

    def place(b, _):
        moment_out[b] = backr[table[2, b]]
        return 0

    lax.fori_loop(0, BLOCKS, place, 0)

    flush(0, send0)
    flush(1, send1)

    @pl.when(few)
    def _():
        remote(sendm.at[0:53], sendm.at[0:53], sent.at[2], recvb, peer).wait_send()

    @pl.when(jnp.logical_not(few))
    def _():
        remote(sendm.at[0:54], sendm.at[0:54], sent.at[2], recvb, peer).wait_send()

    for region in range(3):

        @pl.when(active[region])
        def _():
            took(region, False)

    @pl.when(active[0])
    def _():
        remote(rots.at[0:2], rots.at[0:2], sent.at[6], recvb, peer).wait_send()


def plan(owners, planned):
    shape = (PANEL, PANEL)
    sub = lax.broadcasted_iota(jnp.int32, shape, 0)
    lane = lax.broadcasted_iota(jnp.int32, shape, 1)
    row = jnp.broadcast_to(
        jnp.concatenate([owners[...], jnp.full((1, PANEL - BLOCKS), -1, jnp.int32)], axis=1), shape
    )
    column = row.T

    def across(x):
        return jnp.broadcast_to(jnp.sum(x.astype(jnp.int32), axis=1, keepdims=True), shape)

    def down(x):
        return jnp.broadcast_to(jnp.sum(x.astype(jnp.int32), axis=0, keepdims=True), shape)

    def resting(t):
        return ((t & 1) == 1) & (((t >> 1) & 3) == (t >> 4))

    same = column == row
    rank_c = across(same & (lane < sub))
    rank_r = down(same & (sub < lane))
    mine = column == lane
    first = mine & (rank_c == 0)
    second = mine & (rank_c == 1)
    owned_r = down(mine)
    owned_c = across(row == sub)
    vacant_r = (owned_r == 0) & jnp.logical_not(resting(lane)) & (lane < SHARES)
    vacant_c = (owned_c == 0) & jnp.logical_not(resting(sub)) & (sub < SHARES)
    guest_c = (column >= 0) & ((rank_c == 1) | resting(column))
    guest_r = (row >= 0) & ((rank_r == 1) | resting(row))
    vacant_at = down(vacant_c & (sub < lane))
    guest_at = across(guest_r & (lane < sub))
    hosted = guest_c & vacant_r & (vacant_at == guest_at)
    zero = jnp.zeros(shape, jnp.int32)
    moved = hosted | (first & jnp.logical_not(resting(lane)))
    rows = (
        down(jnp.where(first | hosted, sub, zero)),
        down(jnp.where(second, sub, zero)),
        across(jnp.where(moved, lane, zero)).T,
        owned_r,
        down(second),
    )
    planned[...] = jnp.zeros(planned.shape, jnp.int32)
    for i, x in enumerate(rows):
        planned[i:i + 1, :] = x[0:1, :]


def per_device(factor, old_basis, moment, owner_table):
    bf16 = jnp.bfloat16
    vmem = pl.BlockSpec(memory_space=pltpu.VMEM)
    hbm = pl.BlockSpec(memory_space=pl.ANY)
    return pl.pallas_call(
        refresh_kernel,
        out_shape=(
            jax.ShapeDtypeStruct(moment.shape, bf16),
            jax.ShapeDtypeStruct((1, SLOTS, ORDER, ORDER), bf16),
        ),
        in_specs=[vmem, hbm, hbm, hbm],
        out_specs=(vmem, vmem),
        scratch_shapes=[
            pltpu.VMEM((SHARES, 8, WIDTHS[0][0]), bf16),
            pltpu.VMEM((SHARES, 8, WIDTHS[1][0]), bf16),
            pltpu.VMEM((SHARES, 16, ORDER), bf16),
            pltpu.VMEM((SHARES, 8, WIDTHS[0][0]), bf16),
            pltpu.VMEM((SHARES, 8, WIDTHS[1][0]), bf16),
            pltpu.VMEM((72, 16, ORDER), bf16),
            pltpu.VMEM((72, 16, ORDER), bf16),
            pltpu.VMEM((SHARES, 16, ORDER), bf16),
            pltpu.VMEM((ORDER, ORDER), bf16),
            pltpu.VMEM((ORDER, 2 * ORDER), jnp.float32),
            pltpu.VMEM((PANEL, PANEL), jnp.float32),
            pltpu.VMEM((PANEL, PANEL), jnp.float32),
            pltpu.VMEM((3, ORDER, ORDER), bf16),
            pltpu.VMEM(factor.shape, bf16),
            pltpu.VMEM(old_basis.shape, bf16),
            pltpu.VMEM(moment.shape, bf16),
            pltpu.VMEM((8, PANEL), jnp.int32),
            pltpu.SMEM((8, PANEL), jnp.int32),
            pltpu.SemaphoreType.DMA((7,)),
            pltpu.SemaphoreType.DMA((2,)),
            pltpu.SemaphoreType.DMA((2,)),
            pltpu.SemaphoreType.DMA((3,)),
            pltpu.SemaphoreType.DMA((2,)),
            pltpu.SemaphoreType.DMA,
            pltpu.SemaphoreType.DMA((4,)),
        ],
        compiler_params=pltpu.CompilerParams(
            collective_id=0, has_side_effects=True, vmem_limit_bytes=60 * 2**20
        ),
        cost_estimate=pl.CostEstimate(flops=8 * 10**9, bytes_accessed=4 * 2**20, transcendentals=0),
    )(owner_table.reshape(1, BLOCKS), factor, old_basis, moment)


def solution(mesh):
    in_specs = (
        P("layer", ("fsdp", "own"), None),
        P("layer", ("fsdp", "own"), None),
        P("layer", ("fsdp", "own"), None),
        P("layer", None),
    )
    out_specs = (P("layer", ("fsdp", "own"), None), P("layer", ("fsdp", "own"), None, None))
    return jax.shard_map(
        per_device, mesh=mesh, in_specs=in_specs, out_specs=out_specs, check_vma=False
    )
```

```python
import functools

import jax
import jax.numpy as jnp
from jax import lax
from jax.experimental import pallas as pl
from jax.experimental.pallas import tpu as pltpu
from jax.sharding import PartitionSpec as P

SLOTS = 2
SHARES = 64
BLOCKS = 56
ORDER = 512
PANEL = 128
WIDTHS = ((ORDER + 3 * PANEL, ORDER + 2 * PANEL), (ORDER + 2 * PANEL, ORDER + PANEL))
SUB = 32


def rows_of(v, s):
    return jnp.broadcast_to(v[s:s + 1, :], (8, 128))


def split(x):
    high = x.astype(jnp.bfloat16)
    return high, (x - high.astype(jnp.float32)).astype(jnp.bfloat16)


def left(x, axis):
    high, low = split(x)
    return jnp.concatenate([high, high, low], axis=axis)


def right(x):
    high, low = split(x)
    return jnp.concatenate([high, low, high], axis=0)


def dot_of(a, b, axis):
    return lax.dot_general(a, b, (((axis,), (0,)), ((), ())), preferred_element_type=jnp.float32)


def inverse_of(x):
    r = pl.reciprocal(x, approx=True)
    return r * (2.0 - x * r)


def factor_sub(wide, aug, at):
    tiles = SUB // 8
    wide, aug = list(wide), list(aug)
    sub = lax.broadcasted_iota(jnp.int32, (8, 128), 0)
    cols = {}
    for q in range(SUB):
        for t in range(q // 8, tiles):
            cols[q, t] = jnp.broadcast_to(wide[t][:, at + q:at + q + 1], (8, 128))
    diag = [None] * tiles
    mix = [None] * tiles
    for j in range(0, SUB, 2):
        tj, sj = j // 8, j % 8
        a = rows_of(cols[j, tj], sj)
        b = rows_of(cols[j, tj], sj + 1)
        d = rows_of(cols[j + 1, tj], sj + 1)
        det = a * d - b * b
        r = inverse_of(det)
        m0, m1 = {}, {}
        for t in range(tj, tiles):
            c0, c1 = cols[j, t], cols[j + 1, t]
            x0 = c0 * d - c1 * b
            x1 = c1 * a - c0 * b
            if t == tj:
                x0 = jnp.where(sub > sj + 1, x0, 0.0)
                x1 = jnp.where(sub > sj + 1, x1, 0.0)
            m0[t], m1[t] = x0 * r, x1 * r
        for q in range(j + 2, SUB):
            p0 = rows_of(cols[j, q // 8], q % 8)
            p1 = rows_of(cols[j + 1, q // 8], q % 8)
            for t in range(q // 8, tiles):
                cols[q, t] = cols[q, t] - (m0[t] * p0 + m1[t] * p1)
        w0, w1 = rows_of(wide[tj], sj), rows_of(wide[tj], sj + 1)
        x0, x1 = rows_of(aug[tj], sj), rows_of(aug[tj], sj + 1)
        for t in range(tj, tiles):
            wide[t] = wide[t] - m0[t] * w0 - m1[t] * w1
            aug[t] = aug[t] - m0[t] * x0 - m1[t] * x1
        ia = inverse_of(a)
        e = det * ia
        mu = b * ia
        if sj == 0:
            diag[tj] = jnp.where(sub == 0, a, e)
            mix[tj] = jnp.where(sub == 1, mu, 0.0)
        else:
            diag[tj] = jnp.where(sub == sj, a, jnp.where(sub == sj + 1, e, diag[tj]))
            mix[tj] = jnp.where(sub == sj + 1, mu, mix[tj])
    for t in range(tiles):
        s = lax.rsqrt(diag[t])
        wide[t] = s * (wide[t] - mix[t] * pltpu.roll(wide[t], 1, 0))
        aug[t] = s * (aug[t] - mix[t] * pltpu.roll(aug[t], 1, 0))
    return wide, aug


def dot_t(a, b):
    return dot_of(left(a, 0), right(b), 0)


def factor_block(diags, augs):
    r = lax.broadcasted_iota(jnp.int32, (128, 128), 0)
    c = lax.broadcasted_iota(jnp.int32, (128, 128), 1)
    for x in augs:
        x[...] = (r == c).astype(jnp.float32)
    for i in range(128 // SUB):
        for s, x in zip(diags, augs):
            at = SUB * i
            wide = [s[at + 8 * t:at + 8 * t + 8, :] for t in range(SUB // 8)]
            aug = [x[at + 8 * t:at + 8 * t + 8, :] for t in range(SUB // 8)]
            wide, aug = factor_sub(wide, aug, at)
            for t in range(SUB // 8):
                x[at + 8 * t:at + 8 * t + 8, :] = aug[t]
            if i < 128 // SUB - 1:
                u = jnp.concatenate(wide, axis=0)
                both = right(jnp.concatenate([u, jnp.concatenate(aug, axis=0)], axis=1))
                turned = left(u, 0)
                nx = at + SUB
                upd = dot_of(turned[:, nx:], both, 0)
                s[nx:, :] = s[nx:, :] - upd[:, :128]
                x[nx:, :] = x[nx:, :] - upd[:, 128:]


def at_share(t):
    return {"fsdp": t // 2, "own": lax.rem(t, 2)}


def share(x, y, c):
    return x * 16 + lax.rem(y + 8, 8) * 2 + c


def remote(src, dst, send, recv, t):
    return pltpu.make_async_remote_copy(
        src_ref=src,
        dst_ref=dst,
        send_sem=send,
        recv_sem=recv,
        device_id=at_share(t),
        device_id_type=pl.DeviceIdType.MESH,
    )


def is_idle(t):
    return (lax.rem(t, 2) == 1) & (lax.rem(t // 2, 4) == t // 16)


FIRST = (0, 1, 5)


def wide_f32(x):
    return x.astype(jnp.float32).reshape(-1, x.shape[-1])


def refresh_kernel(
    owners,
    factor_hbm,
    basis_hbm,
    moment_hbm,
    backr,
    owner_basis,
    planned,
    send0,
    send1,
    sendm,
    got0,
    got1,
    gotm,
    backs,
    kept,
    old,
    work,
    diag,
    inverse,
    rots,
    factor,
    basis,
    moment,
    table,
    sent,
    recv0,
    recv1,
    recvm,
    recvr,
    recvb,
    local,
):
    fetches = [
        pltpu.make_async_copy(src, dst, local.at[i])
        for i, (src, dst) in enumerate(
            ((basis_hbm, basis), (factor_hbm, factor), (moment_hbm, moment))
        )
    ]
    for fetch in fetches:
        fetch.start()
    stores = [
        pltpu.make_async_copy(kept.at[slot], owner_basis.at[0, slot], local.at[4 + slot])
        for slot in range(SLOTS)
    ]

    me = lax.axis_index("fsdp") * 2 + lax.axis_index("own")
    panel = me // 16
    line = lax.rem(me // 2, 8)
    core = lax.rem(me, 2)
    seat = panel * 2 + core
    peer = lax.rem(me + 1, SHARES)
    hosts = (me, share(panel, line - 1, core), share(panel, line + 1, core))
    active = [jnp.logical_not(is_idle(t)) for t in hosts]
    few = active[0] & active[1] & active[2]
    short = ((panel < 2) & (core == 1), (panel >= 2) & (core == 0))

    barrier = pltpu.get_barrier_semaphore()

    def greet(k, _):
        pl.semaphore_signal(
            barrier,
            inc=1,
            device_id=at_share(lax.rem(me + k, SHARES)),
            device_id_type=pl.DeviceIdType.MESH,
        )
        return 0

    lax.fori_loop(1, SHARES, greet, 0)

    plan(owners, planned)
    tables = pltpu.make_async_copy(planned, table, local.at[3])
    tables.start()
    for fetch in fetches[:2]:
        fetch.wait()
    tables.wait()

    def piece(b, turn):
        lane = pl.multiple_of(lax.rem(panel + turn, 4) * PANEL, PANEL)
        return factor[b, :, pl.ds(lane, PANEL)]

    tile_lane = lax.broadcasted_iota(jnp.int32, (8, PANEL), 1)
    odd = ((tile_lane >> 3) & 1) == 1
    whole_diag = jnp.logical_not(odd) | (jnp.full((8, PANEL), core, jnp.int32) == 1)
    whole_far = odd | (jnp.full((8, PANEL), panel, jnp.int32) < 2)

    def merge(mask, mine, other, turn):
        turned = pltpu.roll(other.astype(jnp.float32), turn, 1)
        return jnp.where(mask, mine.astype(jnp.float32), turned).astype(jnp.bfloat16)

    def pack0(t):
        a, b = table[0, t], table[1, t]
        send0[t, :, :ORDER] = basis[a]
        send0[t, :, ORDER:ORDER + PANEL] = piece(a, 1)
        send0[t, :, ORDER + PANEL:ORDER + 2 * PANEL] = merge(whole_diag, piece(a, 0), piece(b, 0), 8)
        send0[t, :, ORDER + 2 * PANEL:] = merge(whole_far, piece(a, 2), piece(b, 2), PANEL - 8)

    def pack1(t):
        b = table[1, t]
        send1[t, :, :ORDER] = basis[b]
        send1[t, :, ORDER:ORDER + PANEL] = piece(b, 1)
        send1[t, :, ORDER + PANEL:] = piece(b, 2 * (1 - core))

    def post(slot, pack, send, got, recv):
        long_width, short_width = WIDTHS[slot]

        def body(k, _):
            t = lax.rem(me + k, SHARES)
            pack(t)

            @pl.when(jnp.logical_not(short[slot]))
            def _():
                remote(send.at[t], got.at[me], sent.at[slot], recv.at[0], t).start()

            @pl.when(short[slot])
            def _():
                remote(
                    send.at[t, :, :short_width],
                    got.at[me, :, :short_width],
                    sent.at[slot],
                    recv.at[1],
                    t,
                ).start()

            return 0

        lax.fori_loop(1, SHARES, body, 0)
        pack(me)
        got[me] = send[me]

    def arrive(slot, got, recv):
        long_width, short_width = WIDTHS[slot]

        def take(longs, shorts):
            part = got.at[0:longs]
            remote(part, part, recv.at[0], recv.at[0], peer).wait_recv()
            part = got.at[0:shorts, :, :short_width]
            remote(part, part, recv.at[1], recv.at[1], peer).wait_recv()

        @pl.when(jnp.logical_not(short[slot]))
        def _():
            take(47, 16)

        @pl.when(short[slot])
        def _():
            take(48, 15)

    def flush(slot, send):
        long_width, short_width = WIDTHS[slot]

        @pl.when(jnp.logical_not(short[slot]))
        def _():
            part = send.at[0:63]
            remote(part, part, sent.at[slot], recvb, peer).wait_send()

        @pl.when(short[slot])
        def _():
            part = send.at[0:63, :, :short_width]
            remote(part, part, sent.at[slot], recvb, peer).wait_send()

    def route(t):
        gap = lax.rem(line - lax.rem(t // 2, 8) + 8, 8)
        above = (gap > 0) & ((gap < 4) | ((gap == 4) & (core == 0)))
        region = jnp.where(gap == 0, 0, jnp.where(above, 1, 2))
        dest = share(t // 16, lax.rem(t // 2, 8) + jnp.where(region == 2, 7, region), lax.rem(t, 2))
        place = jnp.where(gap == 0, 0, jnp.where(above, gap, 12 - gap)) * 8 + seat
        return dest, region, place

    def postm(k, _):
        t = lax.rem(me + k, SHARES)
        sendm[t] = moment[table[0, t]]
        dest, region, place = route(t)

        @pl.when((dest != me) & jnp.logical_not(is_idle(t)))
        def _():
            remote(sendm.at[t], gotm.at[place], sent.at[2], recvm.at[region], dest).start()

        return 0

    def load(slot):
        got = (got0, got1)[slot]
        old[...] = wide_f32(got[:, :, :ORDER]).T.astype(jnp.bfloat16)
        row_odd = ((lax.broadcasted_iota(jnp.int32, (PANEL, PANEL), 0) >> 3) & 1) == 1
        lane_odd = ((lax.broadcasted_iota(jnp.int32, (PANEL, PANEL), 1) >> 3) & 1) == 1

        def tile(ref, p, q):
            lo = ORDER + q * PANEL
            return wide_f32(ref[16 * p:16 * p + 16, :, lo:lo + PANEL])

        part = {}
        for p in range(4):
            q = (p + 1) % 4
            part[p, q] = tile(got, p, 0)
            part[q, p] = part[p, q].T
            own = tile(got0, p, 1)
            if slot == 1:
                own = jnp.where(row_odd, tile(got1, p, 1), pltpu.roll(own, PANEL - 8, 1))
            part[p, p] = jnp.where(row_odd | jnp.logical_not(lane_odd), own, own.T)
        for p in range(2):
            near, far = tile(got0, p, 2), tile(got0, p + 2, 2)
            if slot == 1:
                near, far = tile(got1, p, 1), pltpu.roll(far, 8, 1)
            part[p, p + 2] = jnp.where(row_odd, far.T, near)
            part[p + 2, p] = part[p, p + 2].T
        full = jnp.concatenate(
            [jnp.concatenate([part[p, q] for q in range(4)], axis=1) for p in range(4)], axis=0
        ).astype(jnp.bfloat16)
        pt = jnp.dot(old[...], full, preferred_element_type=jnp.float32).astype(jnp.bfloat16)
        work[:, :ORDER] = lax.dot_general(
            pt, pt, (((1,), (1,)), ((), ())), preferred_element_type=jnp.float32
        )
        work[:, ORDER:] = pt.astype(jnp.float32)

    def panel_step(k):
        at = pl.multiple_of(k * PANEL, PANEL)
        diag[...] = work[pl.ds(at, PANEL), pl.ds(at, PANEL)]
        factor_block([diag], [inverse])
        work[pl.ds(at, PANEL), :] = dot_of(
            left(inverse[...], 1), right(work[pl.ds(at, PANEL), :]), 1
        )
        for kk in range(3):

            @pl.when(k == kk)
            def _():
                lo = PANEL * (kk + 1)
                u = work[lo - PANEL:lo, lo:ORDER]
                work[lo:, lo:] = work[lo:, lo:] - dot_t(u, work[lo - PANEL:lo, lo:])

    def keep(slot):
        there = jnp.full((ORDER, ORDER), table[3 + slot, me], jnp.int32)
        kept[slot] = jnp.where(there > 0, work[:, ORDER:].T, 0.0).astype(jnp.bfloat16)
        stores[slot].start()

    def turn(k):
        at = pl.multiple_of(k * PANEL, PANEL)
        rots[0, k] = lax.dot_general(
            old[...],
            work[pl.ds(at, PANEL), ORDER:].astype(jnp.bfloat16),
            (((1,), (1,)), ((), ())),
            preferred_element_type=jnp.float32,
        ).astype(jnp.bfloat16)
        for side in range(2):
            remote(
                rots.at[0, k], rots.at[2 - side, k], sent.at[6], recvr.at[1 - side, k], hosts[1 + side]
            ).start()

    def turned(region, half):
        for k in (2 * half, 2 * half + 1):
            remote(
                rots.at[0, k], rots.at[region, k], sent.at[6], recvr.at[region - 1, k], peer
            ).wait_recv()

    def local_reply(region, half):
        return pltpu.make_async_copy(
            backs.at[half, FIRST[region] * 8 + seat],
            backr.at[half, hosts[region]],
            local.at[6 + 2 * region + half],
        )

    def rotate(region, half, away):
        g = FIRST[region] + away
        rows = pl.ds(pl.multiple_of(g * 8, 8), 8)
        x = gotm[rows].reshape(8 * 16, ORDER)
        r = jnp.concatenate([rots[region, 2 * half], rots[region, 2 * half + 1]], axis=1)
        y = jnp.dot(x, r, preferred_element_type=jnp.float32).astype(jnp.bfloat16)
        backs[half, rows] = y.reshape(8, 16, 2 * PANEL)
        place = line + (away if region == 1 else -away)

        def reply(k, _):
            t = share(k // 2, place, lax.rem(k, 2))
            ours = jnp.logical_or(away < 3, lax.rem(k, 2) == region - 1)

            @pl.when((t != me) & ours)
            def _():
                remote(
                    backs.at[half, g * 8 + k],
                    backr.at[half, hosts[region]],
                    sent.at[3 + region],
                    recvb,
                    t,
                ).start()

            return 0

        lax.fori_loop(0, 8, reply, 0)

    def rotate_half(half):
        @pl.when(active[0])
        def _():
            if half == 0:
                took(0, True)
            rotate(0, half, 0)
            local_reply(0, half).start()

        for region in (1, 2):

            @pl.when(active[region])
            def _():
                if half == 0:
                    took(region, True)
                turned(region, half)

        def pair(away, _):
            for region in (1, 2):

                @pl.when(active[region])
                def _():
                    rotate(region, half, away)

            return 0

        lax.fori_loop(0, 4, pair, 0)
        for region in (1, 2):

            @pl.when(active[region])
            def _():
                local_reply(region, half).start()

    def took(region, wait_in):
        count = 7 if region == 0 else 27
        if wait_in:
            part = gotm.at[0:count]
            remote(part, part, sent.at[2], recvm.at[region], peer).wait_recv()
        else:
            part = backs.at[:, 0:count]
            remote(part, part, sent.at[3 + region], recvb, peer).wait_send()

    def post_moments():
        lax.fori_loop(0, SHARES, postm, 0)
        for region in range(3):
            gotm[(0, 8, 40)[region] + seat] = sendm[hosts[region]]

    pl.semaphore_wait(barrier, SHARES - 1)
    post(0, pack0, send0, got0, recv0)
    post(1, pack1, send1, got1, recv1)
    fetches[2].wait()
    post_moments()

    def step(i, _):
        @pl.when(i == 0)
        def _():
            arrive(0, got0, recv0)
            load(0)

        @pl.when(i == 4)
        def _():
            keep(0)

            arrive(1, got1, recv1)
            load(1)

        for half in range(2):

            @pl.when(i == 5 + half)
            def _():
                rotate_half(half)

        panel_step(lax.rem(i, 4))

        @pl.when((i < 4) & active[0])
        def _():
            turn(lax.rem(i, 4))

        return 0

    lax.fori_loop(0, 8, step, 0)
    keep(1)

    @pl.when(few)
    def _():
        part = backr.at[:, 0:53]
        remote(part, part, sent.at[2], recvb, peer).wait_recv()

    @pl.when(jnp.logical_not(few))
    def _():
        part = backr.at[:, 0:54]
        remote(part, part, sent.at[2], recvb, peer).wait_recv()

    flush(0, send0)
    flush(1, send1)

    @pl.when(few)
    def _():
        remote(sendm.at[0:53], sendm.at[0:53], sent.at[2], recvb, peer).wait_send()

    @pl.when(jnp.logical_not(few))
    def _():
        remote(sendm.at[0:54], sendm.at[0:54], sent.at[2], recvb, peer).wait_send()

    for region in range(3):

        @pl.when(active[region])
        def _():
            took(region, False)
            for half in range(2):
                local_reply(region, half).wait()

    for store in stores:
        store.wait()

    @pl.when(active[0])
    def _():
        remote(rots.at[0:2], rots.at[0:2], sent.at[6], recvb, peer).wait_send()


def plan(owners, planned):
    shape = (PANEL, PANEL)
    sub = lax.broadcasted_iota(jnp.int32, shape, 0)
    lane = lax.broadcasted_iota(jnp.int32, shape, 1)
    row = jnp.broadcast_to(
        jnp.concatenate([owners[...], jnp.full((1, PANEL - BLOCKS), -1, jnp.int32)], axis=1), shape
    )
    column = row.T

    def across(x):
        return jnp.broadcast_to(jnp.sum(x.astype(jnp.int32), axis=1, keepdims=True), shape)

    def down(x):
        return jnp.broadcast_to(jnp.sum(x.astype(jnp.int32), axis=0, keepdims=True), shape)

    def resting(t):
        return ((t & 1) == 1) & (((t >> 1) & 3) == (t >> 4))

    same = column == row
    rank_c = across(same & (lane < sub))
    rank_r = down(same & (sub < lane))
    mine = column == lane
    first = mine & (rank_c == 0)
    second = mine & (rank_c == 1)
    owned_r = down(mine)
    owned_c = across(row == sub)
    vacant_r = (owned_r == 0) & jnp.logical_not(resting(lane)) & (lane < SHARES)
    vacant_c = (owned_c == 0) & jnp.logical_not(resting(sub)) & (sub < SHARES)
    guest_c = (column >= 0) & ((rank_c == 1) | resting(column))
    guest_r = (row >= 0) & ((rank_r == 1) | resting(row))
    vacant_at = down(vacant_c & (sub < lane))
    guest_at = across(guest_r & (lane < sub))
    hosted = guest_c & vacant_r & (vacant_at == guest_at)
    zero = jnp.zeros(shape, jnp.int32)
    moved = hosted | (first & jnp.logical_not(resting(lane)))
    rows = (
        down(jnp.where(first | hosted, sub, zero)),
        down(jnp.where(second, sub, zero)),
        across(jnp.where(moved, lane, zero)).T,
        owned_r,
        down(second),
    )
    planned[...] = jnp.zeros(planned.shape, jnp.int32)
    for i, x in enumerate(rows):
        planned[i:i + 1, :] = x[0:1, :]


def place_kernel(table, backs, kept, moment_out, owner_basis, rows, bases, sems):
    parts = SHARES // 16
    loads, bases_in, bases_out = [], [], []
    for q in range(parts):
        cut = slice(16 * q, 16 * q + 16)
        loads.append(pltpu.make_async_copy(backs.at[:, cut], rows.at[:, cut], sems.at[q]))
        loads[q].start()
    for slot in range(SLOTS):
        bases_in.append(
            pltpu.make_async_copy(kept.at[0, slot], bases.at[slot], sems.at[parts + slot])
        )
        bases_out.append(
            pltpu.make_async_copy(
                bases.at[slot], owner_basis.at[0, slot], sems.at[parts + SLOTS + slot]
            )
        )
        bases_in[slot].start()

    def place(t, _):
        @pl.when(jnp.logical_not(is_idle(t)))
        def _():
            for half in range(2):
                pltpu.make_async_copy(
                    rows.at[half, t],
                    moment_out.at[table[0, t], :, 2 * PANEL * half:2 * PANEL * (half + 1)],
                    sems.at[parts + 2 * SLOTS],
                ).start()

        return 0

    for q in range(parts):
        loads[q].wait()
        lax.fori_loop(16 * q, 16 * q + 16, place, 0)
    for slot in range(SLOTS):
        bases_in[slot].wait()
        bases_out[slot].start()
    pltpu.make_async_copy(moment_out, moment_out, sems.at[parts + 2 * SLOTS]).wait()
    for slot in range(SLOTS):
        bases_out[slot].wait()


def per_device(factor, old_basis, moment, owner_table):
    bf16 = jnp.bfloat16
    vmem = pl.BlockSpec(memory_space=pltpu.VMEM)
    hbm = pl.BlockSpec(memory_space=pl.ANY)
    kept = jax.ShapeDtypeStruct((1, SLOTS, ORDER, ORDER), bf16)
    backs, bases, table = pl.pallas_call(
        refresh_kernel,
        out_shape=(
            jax.ShapeDtypeStruct((2, SHARES, 16, 2 * PANEL), bf16),
            kept,
            jax.ShapeDtypeStruct((8, PANEL), jnp.int32),
        ),
        in_specs=[vmem, hbm, hbm, hbm],
        out_specs=(hbm, hbm, vmem),
        scratch_shapes=[
            pltpu.VMEM((SHARES, 8, WIDTHS[0][0]), bf16),
            pltpu.VMEM((SHARES, 8, WIDTHS[1][0]), bf16),
            pltpu.VMEM((SHARES, 16, ORDER), bf16),
            pltpu.VMEM((SHARES, 8, WIDTHS[0][0]), bf16),
            pltpu.VMEM((SHARES, 8, WIDTHS[1][0]), bf16),
            pltpu.VMEM((72, 16, ORDER), bf16),
            pltpu.VMEM((2, 72, 16, 2 * PANEL), bf16),
            pltpu.VMEM((SLOTS, ORDER, ORDER), bf16),
            pltpu.VMEM((ORDER, ORDER), bf16),
            pltpu.VMEM((ORDER, 2 * ORDER), jnp.float32),
            pltpu.VMEM((PANEL, PANEL), jnp.float32),
            pltpu.VMEM((PANEL, PANEL), jnp.float32),
            pltpu.VMEM((3, 4, ORDER, PANEL), bf16),
            pltpu.VMEM(factor.shape, bf16),
            pltpu.VMEM(old_basis.shape, bf16),
            pltpu.VMEM(moment.shape, bf16),
            pltpu.SMEM((8, PANEL), jnp.int32),
            pltpu.SemaphoreType.DMA((7,)),
            pltpu.SemaphoreType.DMA((2,)),
            pltpu.SemaphoreType.DMA((2,)),
            pltpu.SemaphoreType.DMA((3,)),
            pltpu.SemaphoreType.DMA((2, 4)),
            pltpu.SemaphoreType.DMA,
            pltpu.SemaphoreType.DMA((12,)),
        ],
        compiler_params=pltpu.CompilerParams(
            collective_id=0, has_side_effects=True, vmem_limit_bytes=60 * 2**20
        ),
        cost_estimate=pl.CostEstimate(flops=8 * 10**9, bytes_accessed=4 * 2**20, transcendentals=0),
    )(owner_table.reshape(1, BLOCKS), factor, old_basis, moment)
    return pl.pallas_call(
        place_kernel,
        out_shape=(jax.ShapeDtypeStruct(moment.shape, bf16), kept),
        in_specs=[pl.BlockSpec(memory_space=pltpu.SMEM), hbm, hbm],
        out_specs=(hbm, hbm),
        scratch_shapes=[
            pltpu.VMEM(backs.shape, bf16),
            pltpu.VMEM(bases.shape[1:], bf16),
            pltpu.SemaphoreType.DMA((SHARES // 16 + 2 * SLOTS + 1,)),
        ],
        compiler_params=pltpu.CompilerParams(vmem_limit_bytes=60 * 2**20),
    )(table, backs, bases)


def solution(mesh):
    in_specs = (
        P("layer", ("fsdp", "own"), None),
        P("layer", ("fsdp", "own"), None),
        P("layer", ("fsdp", "own"), None),
        P("layer", None),
    )
    out_specs = (P("layer", ("fsdp", "own"), None), P("layer", ("fsdp", "own"), None, None))
    return jax.shard_map(
        per_device, mesh=mesh, in_specs=in_specs, out_specs=out_specs, check_vma=False
    )
```

```python
import functools

import jax
import jax.numpy as jnp
from jax import lax
from jax.experimental import pallas as pl
from jax.experimental.pallas import tpu as pltpu
from jax.sharding import PartitionSpec as P

SLOTS = 2
SHARES = 64
BLOCKS = 56
ORDER = 512
PANEL = 128
WIDTHS = ((ORDER + 3 * PANEL, ORDER + 2 * PANEL), (ORDER + 2 * PANEL, ORDER + PANEL))
SUB = 32


def rows_of(v, s):
    return jnp.broadcast_to(v[s:s + 1, :], (8, 128))


def split(x):
    high = x.astype(jnp.bfloat16)
    return high, (x - high.astype(jnp.float32)).astype(jnp.bfloat16)


def left(x, axis):
    high, low = split(x)
    return jnp.concatenate([high, high, low], axis=axis)


def right(x):
    high, low = split(x)
    return jnp.concatenate([high, low, high], axis=0)


def dot_of(a, b, axis):
    return lax.dot_general(a, b, (((axis,), (0,)), ((), ())), preferred_element_type=jnp.float32)


def inverse_of(x):
    r = pl.reciprocal(x, approx=True)
    return r * (2.0 - x * r)


def factor_sub(wide, aug, at):
    tiles = SUB // 8
    wide, aug = list(wide), list(aug)
    sub = lax.broadcasted_iota(jnp.int32, (8, 128), 0)
    cols = {}
    for q in range(SUB):
        for t in range(q // 8, tiles):
            cols[q, t] = jnp.broadcast_to(wide[t][:, at + q:at + q + 1], (8, 128))
    diag = [None] * tiles
    mix = [None] * tiles
    for j in range(0, SUB, 2):
        tj, sj = j // 8, j % 8
        a = rows_of(cols[j, tj], sj)
        b = rows_of(cols[j, tj], sj + 1)
        d = rows_of(cols[j + 1, tj], sj + 1)
        det = a * d - b * b
        r = inverse_of(det)
        m0, m1 = {}, {}
        for t in range(tj, tiles):
            c0, c1 = cols[j, t], cols[j + 1, t]
            x0 = c0 * d - c1 * b
            x1 = c1 * a - c0 * b
            if t == tj:
                x0 = jnp.where(sub > sj + 1, x0, 0.0)
                x1 = jnp.where(sub > sj + 1, x1, 0.0)
            m0[t], m1[t] = x0 * r, x1 * r
        for q in range(j + 2, SUB):
            p0 = rows_of(cols[j, q // 8], q % 8)
            p1 = rows_of(cols[j + 1, q // 8], q % 8)
            for t in range(q // 8, tiles):
                cols[q, t] = cols[q, t] - (m0[t] * p0 + m1[t] * p1)
        w0, w1 = rows_of(wide[tj], sj), rows_of(wide[tj], sj + 1)
        x0, x1 = rows_of(aug[tj], sj), rows_of(aug[tj], sj + 1)
        for t in range(tj, tiles):
            wide[t] = wide[t] - m0[t] * w0 - m1[t] * w1
            aug[t] = aug[t] - m0[t] * x0 - m1[t] * x1
        ia = inverse_of(a)
        e = det * ia
        mu = b * ia
        if sj == 0:
            diag[tj] = jnp.where(sub == 0, a, e)
            mix[tj] = jnp.where(sub == 1, mu, 0.0)
        else:
            diag[tj] = jnp.where(sub == sj, a, jnp.where(sub == sj + 1, e, diag[tj]))
            mix[tj] = jnp.where(sub == sj + 1, mu, mix[tj])
    for t in range(tiles):
        s = lax.rsqrt(diag[t])
        wide[t] = s * (wide[t] - mix[t] * pltpu.roll(wide[t], 1, 0))
        aug[t] = s * (aug[t] - mix[t] * pltpu.roll(aug[t], 1, 0))
    return wide, aug


def dot_t(a, b):
    return dot_of(left(a, 0), right(b), 0)


def factor_block(diags, augs):
    r = lax.broadcasted_iota(jnp.int32, (128, 128), 0)
    c = lax.broadcasted_iota(jnp.int32, (128, 128), 1)
    for x in augs:
        x[...] = (r == c).astype(jnp.float32)
    for i in range(128 // SUB):
        for s, x in zip(diags, augs):
            at = SUB * i
            wide = [s[at + 8 * t:at + 8 * t + 8, :] for t in range(SUB // 8)]
            aug = [x[at + 8 * t:at + 8 * t + 8, :] for t in range(SUB // 8)]
            wide, aug = factor_sub(wide, aug, at)
            for t in range(SUB // 8):
                x[at + 8 * t:at + 8 * t + 8, :] = aug[t]
            if i < 128 // SUB - 1:
                u = jnp.concatenate(wide, axis=0)
                both = right(jnp.concatenate([u, jnp.concatenate(aug, axis=0)], axis=1))
                turned = left(u, 0)
                nx = at + SUB
                upd = dot_of(turned[:, nx:], both, 0)
                s[nx:, :] = s[nx:, :] - upd[:, :128]
                x[nx:, :] = x[nx:, :] - upd[:, 128:]


def at_share(t):
    return {"fsdp": t // 2, "own": lax.rem(t, 2)}


def share(x, y, c):
    return x * 16 + lax.rem(y + 8, 8) * 2 + c


def remote(src, dst, send, recv, t):
    return pltpu.make_async_remote_copy(
        src_ref=src,
        dst_ref=dst,
        send_sem=send,
        recv_sem=recv,
        device_id=at_share(t),
        device_id_type=pl.DeviceIdType.MESH,
    )


def is_idle(t):
    return (lax.rem(t, 2) == 1) & (lax.rem(t // 2, 4) == t // 16)


FIRST = (0, 1, 5)


def wide_f32(x):
    return x.astype(jnp.float32).reshape(-1, x.shape[-1])


def refresh_kernel(
    owners_hbm,
    factor_hbm,
    basis_hbm,
    moment_hbm,
    backr,
    owner_basis,
    planned,
    send0,
    send1,
    sendm,
    got0,
    got1,
    gotm,
    backs,
    old,
    work,
    diag,
    inverse,
    rots,
    owners,
    factor,
    basis,
    moment,
    table,
    sent,
    recv0,
    recv1,
    recvm,
    recvr,
    recvb,
    local,
):
    fetches = [
        pltpu.make_async_copy(src, dst, local.at[i])
        for i, (src, dst) in enumerate(
            (
                (owners_hbm, owners),
                (basis_hbm, basis),
                (factor_hbm, factor),
                (moment_hbm, moment),
            )
        )
    ]
    for fetch in fetches:
        fetch.start()

    me = lax.axis_index("fsdp") * 2 + lax.axis_index("own")
    panel = me // 16
    line = lax.rem(me // 2, 8)
    core = lax.rem(me, 2)
    seat = panel * 2 + core
    peer = lax.rem(me + 1, SHARES)
    hosts = (me, share(panel, line - 1, core), share(panel, line + 1, core))
    active = [jnp.logical_not(is_idle(t)) for t in hosts]
    few = active[0] & active[1] & active[2]
    short = ((panel < 2) & (core == 1), (panel >= 2) & (core == 0))

    barrier = pltpu.get_barrier_semaphore()

    def greet(k, _):
        pl.semaphore_signal(
            barrier,
            inc=1,
            device_id=at_share(lax.rem(me + k, SHARES)),
            device_id_type=pl.DeviceIdType.MESH,
        )
        return 0

    lax.fori_loop(1, SHARES, greet, 0)

    fetches[0].wait()
    plan(owners, planned)
    tables = pltpu.make_async_copy(planned, table, local.at[4])
    tables.start()
    for fetch in fetches[1:3]:
        fetch.wait()
    tables.wait()

    def piece(b, turn):
        lane = pl.multiple_of(lax.rem(panel + turn, 4) * PANEL, PANEL)
        return factor[b, :, pl.ds(lane, PANEL)]

    tile_lane = lax.broadcasted_iota(jnp.int32, (8, PANEL), 1)
    odd = ((tile_lane >> 3) & 1) == 1
    whole_diag = jnp.logical_not(odd) | (jnp.full((8, PANEL), core, jnp.int32) == 1)
    whole_far = odd | (jnp.full((8, PANEL), panel, jnp.int32) < 2)

    def merge(mask, mine, other, turn):
        turned = pltpu.roll(other.astype(jnp.float32), turn, 1)
        return jnp.where(mask, mine.astype(jnp.float32), turned).astype(jnp.bfloat16)

    def pack0(t):
        a, b = table[0, t], table[1, t]
        send0[t, :, :ORDER] = basis[a]
        send0[t, :, ORDER:ORDER + PANEL] = piece(a, 1)
        send0[t, :, ORDER + PANEL:ORDER + 2 * PANEL] = merge(whole_diag, piece(a, 0), piece(b, 0), 8)
        send0[t, :, ORDER + 2 * PANEL:] = merge(whole_far, piece(a, 2), piece(b, 2), PANEL - 8)

    def pack1(t):
        b = table[1, t]
        send1[t, :, :ORDER] = basis[b]
        send1[t, :, ORDER:ORDER + PANEL] = piece(b, 1)
        send1[t, :, ORDER + PANEL:] = piece(b, 2 * (1 - core))

    def post(slot, pack, send, got, recv):
        long_width, short_width = WIDTHS[slot]

        def body(k, _):
            t = lax.rem(me + k, SHARES)
            pack(t)

            @pl.when(jnp.logical_not(short[slot]))
            def _():
                remote(send.at[t], got.at[me], sent.at[slot], recv.at[0], t).start()

            @pl.when(short[slot])
            def _():
                remote(
                    send.at[t, :, :short_width],
                    got.at[me, :, :short_width],
                    sent.at[slot],
                    recv.at[1],
                    t,
                ).start()

            return 0

        lax.fori_loop(1, SHARES, body, 0)
        pack(me)
        got[me] = send[me]

    def arrive(slot, got, recv):
        long_width, short_width = WIDTHS[slot]

        def take(longs, shorts):
            part = got.at[0:longs]
            remote(part, part, recv.at[0], recv.at[0], peer).wait_recv()
            part = got.at[0:shorts, :, :short_width]
            remote(part, part, recv.at[1], recv.at[1], peer).wait_recv()

        @pl.when(jnp.logical_not(short[slot]))
        def _():
            take(47, 16)

        @pl.when(short[slot])
        def _():
            take(48, 15)

    def flush(slot, send):
        long_width, short_width = WIDTHS[slot]

        @pl.when(jnp.logical_not(short[slot]))
        def _():
            part = send.at[0:63]
            remote(part, part, sent.at[slot], recvb, peer).wait_send()

        @pl.when(short[slot])
        def _():
            part = send.at[0:63, :, :short_width]
            remote(part, part, sent.at[slot], recvb, peer).wait_send()

    def route(t):
        gap = lax.rem(line - lax.rem(t // 2, 8) + 8, 8)
        above = (gap > 0) & ((gap < 4) | ((gap == 4) & (core == 0)))
        region = jnp.where(gap == 0, 0, jnp.where(above, 1, 2))
        dest = share(t // 16, lax.rem(t // 2, 8) + jnp.where(region == 2, 7, region), lax.rem(t, 2))
        place = jnp.where(gap == 0, 0, jnp.where(above, gap, 12 - gap)) * 8 + seat
        return dest, region, place

    def postm(k, _):
        t = lax.rem(me + k, SHARES)
        sendm[t] = moment[table[0, t]]
        dest, region, place = route(t)

        @pl.when((dest != me) & jnp.logical_not(is_idle(t)))
        def _():
            remote(sendm.at[t], gotm.at[place], sent.at[2], recvm.at[region], dest).start()

        return 0

    def load(slot):
        got = (got0, got1)[slot]
        old[...] = wide_f32(got[:, :, :ORDER]).T.astype(jnp.bfloat16)
        row_odd = ((lax.broadcasted_iota(jnp.int32, (PANEL, PANEL), 0) >> 3) & 1) == 1
        lane_odd = ((lax.broadcasted_iota(jnp.int32, (PANEL, PANEL), 1) >> 3) & 1) == 1

        def tile(ref, p, q):
            lo = ORDER + q * PANEL
            return wide_f32(ref[16 * p:16 * p + 16, :, lo:lo + PANEL])

        part = {}
        for p in range(4):
            q = (p + 1) % 4
            part[p, q] = tile(got, p, 0)
            part[q, p] = part[p, q].T
            own = tile(got0, p, 1)
            if slot == 1:
                own = jnp.where(row_odd, tile(got1, p, 1), pltpu.roll(own, PANEL - 8, 1))
            part[p, p] = jnp.where(row_odd | jnp.logical_not(lane_odd), own, own.T)
        for p in range(2):
            near, far = tile(got0, p, 2), tile(got0, p + 2, 2)
            if slot == 1:
                near, far = tile(got1, p, 1), pltpu.roll(far, 8, 1)
            part[p, p + 2] = jnp.where(row_odd, far.T, near)
            part[p + 2, p] = part[p, p + 2].T
        full = jnp.concatenate(
            [jnp.concatenate([part[p, q] for q in range(4)], axis=1) for p in range(4)], axis=0
        ).astype(jnp.bfloat16)
        pt = jnp.dot(old[...], full, preferred_element_type=jnp.float32).astype(jnp.bfloat16)
        work[:, :ORDER] = lax.dot_general(
            pt, pt, (((1,), (1,)), ((), ())), preferred_element_type=jnp.float32
        )
        work[:, ORDER:] = pt.astype(jnp.float32)

    def panel_step(k):
        at = pl.multiple_of(k * PANEL, PANEL)
        diag[...] = work[pl.ds(at, PANEL), pl.ds(at, PANEL)]
        factor_block([diag], [inverse])
        work[pl.ds(at, PANEL), :] = dot_of(
            left(inverse[...], 1), right(work[pl.ds(at, PANEL), :]), 1
        )
        for kk in range(3):

            @pl.when(k == kk)
            def _():
                lo = PANEL * (kk + 1)
                u = work[lo - PANEL:lo, lo:ORDER]
                work[lo:, lo:] = work[lo:, lo:] - dot_t(u, work[lo - PANEL:lo, lo:])

    def keep(slot):
        there = jnp.full((ORDER, ORDER), table[3 + slot, me], jnp.int32)
        owner_basis[0, slot] = jnp.where(there > 0, work[:, ORDER:].T, 0.0).astype(jnp.bfloat16)

    def turn(k):
        at = pl.multiple_of(k * PANEL, PANEL)
        rots[0, k] = lax.dot_general(
            old[...],
            work[pl.ds(at, PANEL), ORDER:].astype(jnp.bfloat16),
            (((1,), (1,)), ((), ())),
            preferred_element_type=jnp.float32,
        ).astype(jnp.bfloat16)
        for side in range(2):
            remote(
                rots.at[0, k], rots.at[2 - side, k], sent.at[6], recvr.at[1 - side, k], hosts[1 + side]
            ).start()

    def turned(region, half):
        for k in (2 * half, 2 * half + 1):
            remote(
                rots.at[0, k], rots.at[region, k], sent.at[6], recvr.at[region - 1, k], peer
            ).wait_recv()

    def local_reply(region, half):
        return pltpu.make_async_copy(
            backs.at[half, FIRST[region] * 8 + seat],
            backr.at[half, hosts[region]],
            local.at[5 + 2 * region + half],
        )

    def rotate(region, half, away):
        g = FIRST[region] + away
        rows = pl.ds(pl.multiple_of(g * 8, 8), 8)
        x = gotm[rows].reshape(8 * 16, ORDER)
        r = jnp.concatenate([rots[region, 2 * half], rots[region, 2 * half + 1]], axis=1)
        y = jnp.dot(x, r, preferred_element_type=jnp.float32).astype(jnp.bfloat16)
        backs[half, rows] = y.reshape(8, 16, 2 * PANEL)
        place = line + (away if region == 1 else -away)

        def reply(k, _):
            t = share(k // 2, place, lax.rem(k, 2))
            ours = jnp.logical_or(away < 3, lax.rem(k, 2) == region - 1)

            @pl.when((t != me) & ours)
            def _():
                remote(
                    backs.at[half, g * 8 + k],
                    backr.at[half, hosts[region]],
                    sent.at[3 + region],
                    recvb,
                    t,
                ).start()

            return 0

        lax.fori_loop(0, 8, reply, 0)

    def rotate_half(half):
        @pl.when(active[0])
        def _():
            if half == 0:
                took(0, True)
            rotate(0, half, 0)
            local_reply(0, half).start()

        for region in (1, 2):

            @pl.when(active[region])
            def _():
                if half == 0:
                    took(region, True)
                turned(region, half)

        def pair(away, _):
            for region in (1, 2):

                @pl.when(active[region])
                def _():
                    rotate(region, half, away)

            return 0

        lax.fori_loop(0, 4, pair, 0)
        for region in (1, 2):

            @pl.when(active[region])
            def _():
                local_reply(region, half).start()

    def took(region, wait_in):
        count = 7 if region == 0 else 27
        if wait_in:
            part = gotm.at[0:count]
            remote(part, part, sent.at[2], recvm.at[region], peer).wait_recv()
        else:
            part = backs.at[:, 0:count]
            remote(part, part, sent.at[3 + region], recvb, peer).wait_send()

    def post_moments():
        lax.fori_loop(0, SHARES, postm, 0)
        for region in range(3):
            gotm[(0, 8, 40)[region] + seat] = sendm[hosts[region]]

    pl.semaphore_wait(barrier, SHARES - 1)
    post(0, pack0, send0, got0, recv0)
    post(1, pack1, send1, got1, recv1)
    fetches[3].wait()
    post_moments()

    def step(i, _):
        @pl.when(i == 0)
        def _():
            arrive(0, got0, recv0)
            load(0)

        @pl.when(i == 4)
        def _():
            keep(0)

            arrive(1, got1, recv1)
            load(1)

        for half in range(2):

            @pl.when(i == 5 + half)
            def _():
                rotate_half(half)

        panel_step(lax.rem(i, 4))

        @pl.when((i < 4) & active[0])
        def _():
            turn(lax.rem(i, 4))

        return 0

    lax.fori_loop(0, 8, step, 0)
    keep(1)

    @pl.when(few)
    def _():
        part = backr.at[:, 0:53]
        remote(part, part, sent.at[2], recvb, peer).wait_recv()

    @pl.when(jnp.logical_not(few))
    def _():
        part = backr.at[:, 0:54]
        remote(part, part, sent.at[2], recvb, peer).wait_recv()

    flush(0, send0)
    flush(1, send1)

    @pl.when(few)
    def _():
        remote(sendm.at[0:53], sendm.at[0:53], sent.at[2], recvb, peer).wait_send()

    @pl.when(jnp.logical_not(few))
    def _():
        remote(sendm.at[0:54], sendm.at[0:54], sent.at[2], recvb, peer).wait_send()

    for region in range(3):

        @pl.when(active[region])
        def _():
            took(region, False)
            for half in range(2):
                local_reply(region, half).wait()

    @pl.when(active[0])
    def _():
        remote(rots.at[0:2], rots.at[0:2], sent.at[6], recvb, peer).wait_send()


def plan(owners, planned):
    shape = (PANEL, PANEL)
    sub = lax.broadcasted_iota(jnp.int32, shape, 0)
    lane = lax.broadcasted_iota(jnp.int32, shape, 1)
    row = jnp.broadcast_to(
        jnp.concatenate([owners[...], jnp.full((1, PANEL - BLOCKS), -1, jnp.int32)], axis=1), shape
    )
    column = row.T

    def across(x):
        return jnp.broadcast_to(jnp.sum(x.astype(jnp.int32), axis=1, keepdims=True), shape)

    def down(x):
        return jnp.broadcast_to(jnp.sum(x.astype(jnp.int32), axis=0, keepdims=True), shape)

    def resting(t):
        return ((t & 1) == 1) & (((t >> 1) & 3) == (t >> 4))

    same = column == row
    rank_c = across(same & (lane < sub))
    rank_r = down(same & (sub < lane))
    mine = column == lane
    first = mine & (rank_c == 0)
    second = mine & (rank_c == 1)
    owned_r = down(mine)
    owned_c = across(row == sub)
    vacant_r = (owned_r == 0) & jnp.logical_not(resting(lane)) & (lane < SHARES)
    vacant_c = (owned_c == 0) & jnp.logical_not(resting(sub)) & (sub < SHARES)
    guest_c = (column >= 0) & ((rank_c == 1) | resting(column))
    guest_r = (row >= 0) & ((rank_r == 1) | resting(row))
    vacant_at = down(vacant_c & (sub < lane))
    guest_at = across(guest_r & (lane < sub))
    hosted = guest_c & vacant_r & (vacant_at == guest_at)
    zero = jnp.zeros(shape, jnp.int32)
    moved = hosted | (first & jnp.logical_not(resting(lane)))
    rows = (
        down(jnp.where(first | hosted, sub, zero)),
        down(jnp.where(second, sub, zero)),
        across(jnp.where(moved, lane, zero)).T,
        owned_r,
        down(second),
    )
    planned[...] = jnp.zeros(planned.shape, jnp.int32)
    for i, x in enumerate(rows):
        planned[i:i + 1, :] = x[0:1, :]


def place_kernel(table, rows, bases, moment_out, owner_basis, sems):
    keeps = []
    for slot in range(SLOTS):
        keeps.append(
            pltpu.make_async_copy(bases.at[0, slot], owner_basis.at[0, slot], sems.at[1 + slot])
        )
        keeps[slot].start()

    def place(b, _):
        for half in range(2):
            pltpu.make_async_copy(
                rows.at[half, table[2, b]],
                moment_out.at[b, :, 2 * PANEL * half:2 * PANEL * (half + 1)],
                sems.at[0],
            ).start()
        return 0

    lax.fori_loop(0, BLOCKS, place, 0)
    pltpu.make_async_copy(moment_out, moment_out, sems.at[0]).wait()
    for keep in keeps:
        keep.wait()


def per_device(factor, old_basis, moment, owner_table):
    bf16 = jnp.bfloat16
    vmem = pl.BlockSpec(memory_space=pltpu.VMEM)
    hbm = pl.BlockSpec(memory_space=pl.ANY)
    kept = jax.ShapeDtypeStruct((1, SLOTS, ORDER, ORDER), bf16)
    table = owner_table.reshape(1, BLOCKS)
    held = [
        pltpu.with_memory_space_constraint(x, pltpu.HBM)
        for x in (table, factor, old_basis, moment)
    ]
    backs, bases, table = pl.pallas_call(
        refresh_kernel,
        out_shape=(
            jax.ShapeDtypeStruct((2, SHARES, 16, 2 * PANEL), bf16),
            kept,
            jax.ShapeDtypeStruct((8, PANEL), jnp.int32),
        ),
        in_specs=[hbm] * 4,
        out_specs=(vmem, vmem, vmem),
        scratch_shapes=[
            pltpu.VMEM((SHARES, 8, WIDTHS[0][0]), bf16),
            pltpu.VMEM((SHARES, 8, WIDTHS[1][0]), bf16),
            pltpu.VMEM((SHARES, 16, ORDER), bf16),
            pltpu.VMEM((SHARES, 8, WIDTHS[0][0]), bf16),
            pltpu.VMEM((SHARES, 8, WIDTHS[1][0]), bf16),
            pltpu.VMEM((72, 16, ORDER), bf16),
            pltpu.VMEM((2, 72, 16, 2 * PANEL), bf16),
            pltpu.VMEM((ORDER, ORDER), bf16),
            pltpu.VMEM((ORDER, 2 * ORDER), jnp.float32),
            pltpu.VMEM((PANEL, PANEL), jnp.float32),
            pltpu.VMEM((PANEL, PANEL), jnp.float32),
            pltpu.VMEM((3, 4, ORDER, PANEL), bf16),
            pltpu.VMEM(table.shape, jnp.int32),
            pltpu.VMEM(factor.shape, bf16),
            pltpu.VMEM(old_basis.shape, bf16),
            pltpu.VMEM(moment.shape, bf16),
            pltpu.SMEM((8, PANEL), jnp.int32),
            pltpu.SemaphoreType.DMA((7,)),
            pltpu.SemaphoreType.DMA((2,)),
            pltpu.SemaphoreType.DMA((2,)),
            pltpu.SemaphoreType.DMA((3,)),
            pltpu.SemaphoreType.DMA((2, 4)),
            pltpu.SemaphoreType.DMA,
            pltpu.SemaphoreType.DMA((12,)),
        ],
        compiler_params=pltpu.CompilerParams(
            collective_id=0, has_side_effects=True, vmem_limit_bytes=40 * 2**20
        ),
        cost_estimate=pl.CostEstimate(flops=8 * 10**9, bytes_accessed=4 * 2**20, transcendentals=0),
    )(*held)
    return pl.pallas_call(
        place_kernel,
        out_shape=(jax.ShapeDtypeStruct(moment.shape, bf16), kept),
        in_specs=[pl.BlockSpec(memory_space=pltpu.SMEM), vmem, vmem],
        out_specs=(hbm, hbm),
        scratch_shapes=[pltpu.SemaphoreType.DMA((1 + SLOTS,))],
        compiler_params=pltpu.CompilerParams(vmem_limit_bytes=16 * 2**20),
    )(table, backs, bases)


def solution(mesh):
    in_specs = (
        P("layer", ("fsdp", "own"), None),
        P("layer", ("fsdp", "own"), None),
        P("layer", ("fsdp", "own"), None),
        P("layer", None),
    )
    out_specs = (P("layer", ("fsdp", "own"), None), P("layer", ("fsdp", "own"), None, None))
    return jax.shard_map(
        per_device, mesh=mesh, in_specs=in_specs, out_specs=out_specs, check_vma=False
    )
```

```python
import functools

import jax
import jax.numpy as jnp
from jax import lax
from jax.experimental import pallas as pl
from jax.experimental.pallas import tpu as pltpu
from jax.sharding import PartitionSpec as P

SLOTS = 2
SHARES = 64
BLOCKS = 56
ORDER = 512
PANEL = 128
WIDTHS = ((ORDER + 3 * PANEL, ORDER + 2 * PANEL), (ORDER + 2 * PANEL, ORDER + PANEL))
SUB = 32


def rows_of(v, s):
    return jnp.broadcast_to(v[s:s + 1, :], (8, 128))


def split(x):
    high = x.astype(jnp.bfloat16)
    return high, (x - high.astype(jnp.float32)).astype(jnp.bfloat16)


def left(x, axis):
    high, low = split(x)
    return jnp.concatenate([high, high, low], axis=axis)


def right(x):
    high, low = split(x)
    return jnp.concatenate([high, low, high], axis=0)


def dot_of(a, b, axis):
    return lax.dot_general(a, b, (((axis,), (0,)), ((), ())), preferred_element_type=jnp.float32)


def inverse_of(x):
    r = pl.reciprocal(x, approx=True)
    return r * (2.0 - x * r)


def factor_sub(wide, aug, at):
    tiles = SUB // 8
    wide, aug = list(wide), list(aug)
    sub = lax.broadcasted_iota(jnp.int32, (8, 128), 0)
    cols = {}
    for q in range(SUB):
        for t in range(q // 8, tiles):
            cols[q, t] = jnp.broadcast_to(wide[t][:, at + q:at + q + 1], (8, 128))
    diag = [None] * tiles
    mix = [None] * tiles
    for j in range(0, SUB, 2):
        tj, sj = j // 8, j % 8
        a = rows_of(cols[j, tj], sj)
        b = rows_of(cols[j, tj], sj + 1)
        d = rows_of(cols[j + 1, tj], sj + 1)
        det = a * d - b * b
        r = inverse_of(det)
        m0, m1 = {}, {}
        for t in range(tj, tiles):
            c0, c1 = cols[j, t], cols[j + 1, t]
            x0 = c0 * d - c1 * b
            x1 = c1 * a - c0 * b
            if t == tj:
                x0 = jnp.where(sub > sj + 1, x0, 0.0)
                x1 = jnp.where(sub > sj + 1, x1, 0.0)
            m0[t], m1[t] = x0 * r, x1 * r
        for q in range(j + 2, SUB):
            p0 = rows_of(cols[j, q // 8], q % 8)
            p1 = rows_of(cols[j + 1, q // 8], q % 8)
            for t in range(q // 8, tiles):
                cols[q, t] = cols[q, t] - (m0[t] * p0 + m1[t] * p1)
        w0, w1 = rows_of(wide[tj], sj), rows_of(wide[tj], sj + 1)
        x0, x1 = rows_of(aug[tj], sj), rows_of(aug[tj], sj + 1)
        for t in range(tj, tiles):
            wide[t] = wide[t] - m0[t] * w0 - m1[t] * w1
            aug[t] = aug[t] - m0[t] * x0 - m1[t] * x1
        ia = inverse_of(a)
        e = det * ia
        mu = b * ia
        if sj == 0:
            diag[tj] = jnp.where(sub == 0, a, e)
            mix[tj] = jnp.where(sub == 1, mu, 0.0)
        else:
            diag[tj] = jnp.where(sub == sj, a, jnp.where(sub == sj + 1, e, diag[tj]))
            mix[tj] = jnp.where(sub == sj + 1, mu, mix[tj])
    for t in range(tiles):
        s = lax.rsqrt(diag[t])
        wide[t] = s * (wide[t] - mix[t] * pltpu.roll(wide[t], 1, 0))
        aug[t] = s * (aug[t] - mix[t] * pltpu.roll(aug[t], 1, 0))
    return wide, aug


def dot_t(a, b):
    return dot_of(left(a, 0), right(b), 0)


def factor_block(diags, augs):
    r = lax.broadcasted_iota(jnp.int32, (128, 128), 0)
    c = lax.broadcasted_iota(jnp.int32, (128, 128), 1)
    for x in augs:
        x[...] = (r == c).astype(jnp.float32)
    for i in range(128 // SUB):
        for s, x in zip(diags, augs):
            at = SUB * i
            wide = [s[at + 8 * t:at + 8 * t + 8, :] for t in range(SUB // 8)]
            aug = [x[at + 8 * t:at + 8 * t + 8, :] for t in range(SUB // 8)]
            wide, aug = factor_sub(wide, aug, at)
            for t in range(SUB // 8):
                x[at + 8 * t:at + 8 * t + 8, :] = aug[t]
            if i < 128 // SUB - 1:
                u = jnp.concatenate(wide, axis=0)
                both = right(jnp.concatenate([u, jnp.concatenate(aug, axis=0)], axis=1))
                turned = left(u, 0)
                nx = at + SUB
                upd = dot_of(turned[:, nx:], both, 0)
                s[nx:, :] = s[nx:, :] - upd[:, :128]
                x[nx:, :] = x[nx:, :] - upd[:, 128:]


def at_share(t):
    return {"fsdp": t // 2, "own": lax.rem(t, 2)}


def share(x, y, c):
    return x * 16 + lax.rem(y + 8, 8) * 2 + c


def remote(src, dst, send, recv, t):
    return pltpu.make_async_remote_copy(
        src_ref=src,
        dst_ref=dst,
        send_sem=send,
        recv_sem=recv,
        device_id=at_share(t),
        device_id_type=pl.DeviceIdType.MESH,
    )


def is_idle(t):
    return (lax.rem(t, 2) == 1) & (lax.rem(t // 2, 4) == t // 16)


FIRST = (0, 1, 5)


def wide_f32(x):
    return x.astype(jnp.float32).reshape(-1, x.shape[-1])


def refresh_kernel(
    owners_hbm,
    factor_hbm,
    basis_hbm,
    moment_hbm,
    backr,
    owner_basis,
    planned,
    send0,
    send1,
    sendm,
    got0,
    got1,
    gotm,
    backs,
    old,
    work,
    diag,
    inverse,
    rots,
    owners,
    factor,
    basis,
    moment,
    table,
    sent,
    recv0,
    recv1,
    recvm,
    recvr,
    recvb,
    local,
):
    fetches = [
        pltpu.make_async_copy(src, dst, local.at[i])
        for i, (src, dst) in enumerate(
            (
                (owners_hbm, owners),
                (basis_hbm, basis),
                (factor_hbm, factor),
                (moment_hbm, moment),
            )
        )
    ]
    for fetch in fetches:
        fetch.start()

    me = lax.axis_index("fsdp") * 2 + lax.axis_index("own")
    panel = me // 16
    line = lax.rem(me // 2, 8)
    core = lax.rem(me, 2)
    seat = panel * 2 + core
    peer = lax.rem(me + 1, SHARES)
    hosts = (me, share(panel, line - 1, core), share(panel, line + 1, core))
    active = [jnp.logical_not(is_idle(t)) for t in hosts]
    few = active[0] & active[1] & active[2]
    short = ((panel < 2) & (core == 1), (panel >= 2) & (core == 0))

    barrier = pltpu.get_barrier_semaphore()

    def greet(k, _):
        pl.semaphore_signal(
            barrier,
            inc=1,
            device_id=at_share(lax.rem(me + k, SHARES)),
            device_id_type=pl.DeviceIdType.MESH,
        )
        return 0

    lax.fori_loop(1, SHARES, greet, 0)

    fetches[0].wait()
    plan(owners, planned)
    tables = pltpu.make_async_copy(planned, table, local.at[4])
    tables.start()
    for fetch in fetches[1:3]:
        fetch.wait()
    tables.wait()

    def piece(b, turn):
        lane = pl.multiple_of(lax.rem(panel + turn, 4) * PANEL, PANEL)
        return factor[b, :, pl.ds(lane, PANEL)]

    tile_lane = lax.broadcasted_iota(jnp.int32, (8, PANEL), 1)
    odd = ((tile_lane >> 3) & 1) == 1
    whole_diag = jnp.logical_not(odd) | (jnp.full((8, PANEL), core, jnp.int32) == 1)
    whole_far = odd | (jnp.full((8, PANEL), panel, jnp.int32) < 2)

    def merge(mask, mine, other, turn):
        turned = pltpu.roll(other.astype(jnp.float32), turn, 1)
        return jnp.where(mask, mine.astype(jnp.float32), turned).astype(jnp.bfloat16)

    def pack0(t):
        a, b = table[0, t], table[1, t]
        send0[t, :, :ORDER] = basis[a]
        send0[t, :, ORDER:ORDER + PANEL] = piece(a, 1)
        send0[t, :, ORDER + PANEL:ORDER + 2 * PANEL] = merge(whole_diag, piece(a, 0), piece(b, 0), 8)
        send0[t, :, ORDER + 2 * PANEL:] = merge(whole_far, piece(a, 2), piece(b, 2), PANEL - 8)

    def pack1(t):
        b = table[1, t]
        send1[t, :, :ORDER] = basis[b]
        send1[t, :, ORDER:ORDER + PANEL] = piece(b, 1)
        send1[t, :, ORDER + PANEL:] = piece(b, 2 * (1 - core))

    def post(slot, pack, send, got, recv):
        long_width, short_width = WIDTHS[slot]

        def body(k, _):
            t = lax.rem(me + k, SHARES)
            pack(t)

            @pl.when(jnp.logical_not(short[slot]))
            def _():
                remote(send.at[t], got.at[me], sent.at[slot], recv.at[0], t).start()

            @pl.when(short[slot])
            def _():
                remote(
                    send.at[t, :, :short_width],
                    got.at[me, :, :short_width],
                    sent.at[slot],
                    recv.at[1],
                    t,
                ).start()

            return 0

        lax.fori_loop(1, SHARES, body, 0)
        pack(me)
        got[me] = send[me]

    def arrive(slot, got, recv):
        long_width, short_width = WIDTHS[slot]

        def take(longs, shorts):
            part = got.at[0:longs]
            remote(part, part, recv.at[0], recv.at[0], peer).wait_recv()
            part = got.at[0:shorts, :, :short_width]
            remote(part, part, recv.at[1], recv.at[1], peer).wait_recv()

        @pl.when(jnp.logical_not(short[slot]))
        def _():
            take(47, 16)

        @pl.when(short[slot])
        def _():
            take(48, 15)

    def flush(slot, send):
        long_width, short_width = WIDTHS[slot]

        @pl.when(jnp.logical_not(short[slot]))
        def _():
            part = send.at[0:63]
            remote(part, part, sent.at[slot], recvb, peer).wait_send()

        @pl.when(short[slot])
        def _():
            part = send.at[0:63, :, :short_width]
            remote(part, part, sent.at[slot], recvb, peer).wait_send()

    def route(t):
        gap = lax.rem(line - lax.rem(t // 2, 8) + 8, 8)
        above = (gap > 0) & ((gap < 4) | ((gap == 4) & (core == 0)))
        region = jnp.where(gap == 0, 0, jnp.where(above, 1, 2))
        dest = share(t // 16, lax.rem(t // 2, 8) + jnp.where(region == 2, 7, region), lax.rem(t, 2))
        place = jnp.where(gap == 0, 0, jnp.where(above, gap, 12 - gap)) * 8 + seat
        return dest, region, place

    def postm(k, _):
        t = lax.rem(me + k, SHARES)
        sendm[t] = moment[table[0, t]]
        dest, region, place = route(t)

        @pl.when((dest != me) & jnp.logical_not(is_idle(t)))
        def _():
            remote(sendm.at[t], gotm.at[place], sent.at[2], recvm.at[region], dest).start()

        return 0

    def load(slot):
        got = (got0, got1)[slot]
        old[...] = wide_f32(got[:, :, :ORDER]).T.astype(jnp.bfloat16)
        row_odd = ((lax.broadcasted_iota(jnp.int32, (PANEL, PANEL), 0) >> 3) & 1) == 1
        lane_odd = ((lax.broadcasted_iota(jnp.int32, (PANEL, PANEL), 1) >> 3) & 1) == 1

        def tile(ref, p, q):
            lo = ORDER + q * PANEL
            return wide_f32(ref[16 * p:16 * p + 16, :, lo:lo + PANEL])

        part = {}
        for p in range(4):
            q = (p + 1) % 4
            part[p, q] = tile(got, p, 0)
            part[q, p] = part[p, q].T
            own = tile(got0, p, 1)
            if slot == 1:
                own = jnp.where(row_odd, tile(got1, p, 1), pltpu.roll(own, PANEL - 8, 1))
            part[p, p] = jnp.where(row_odd | jnp.logical_not(lane_odd), own, own.T)
        for p in range(2):
            near, far = tile(got0, p, 2), tile(got0, p + 2, 2)
            if slot == 1:
                near, far = tile(got1, p, 1), pltpu.roll(far, 8, 1)
            part[p, p + 2] = jnp.where(row_odd, far.T, near)
            part[p + 2, p] = part[p, p + 2].T
        full = jnp.concatenate(
            [jnp.concatenate([part[p, q] for q in range(4)], axis=1) for p in range(4)], axis=0
        ).astype(jnp.bfloat16)
        pt = jnp.dot(old[...], full, preferred_element_type=jnp.float32).astype(jnp.bfloat16)
        work[:, :ORDER] = lax.dot_general(
            pt, pt, (((1,), (1,)), ((), ())), preferred_element_type=jnp.float32
        )
        work[:, ORDER:] = pt.astype(jnp.float32)

    def panel_step(k):
        at = pl.multiple_of(k * PANEL, PANEL)
        diag[...] = work[pl.ds(at, PANEL), pl.ds(at, PANEL)]
        factor_block([diag], [inverse])
        work[pl.ds(at, PANEL), :] = dot_of(
            left(inverse[...], 1), right(work[pl.ds(at, PANEL), :]), 1
        )
        for kk in range(3):

            @pl.when(k == kk)
            def _():
                lo = PANEL * (kk + 1)
                u = work[lo - PANEL:lo, lo:ORDER]
                work[lo:, lo:] = work[lo:, lo:] - dot_t(u, work[lo - PANEL:lo, lo:])

    def keep(slot):
        there = jnp.full((ORDER, ORDER), table[3 + slot, me], jnp.int32)
        owner_basis[0, slot] = jnp.where(there > 0, work[:, ORDER:].T, 0.0).astype(jnp.bfloat16)

    def turn(k):
        at = pl.multiple_of(k * PANEL, PANEL)
        rots[0, k] = lax.dot_general(
            old[...],
            work[pl.ds(at, PANEL), ORDER:].astype(jnp.bfloat16),
            (((1,), (1,)), ((), ())),
            preferred_element_type=jnp.float32,
        ).astype(jnp.bfloat16)
        for side in range(2):
            remote(
                rots.at[0, k], rots.at[2 - side, k], sent.at[6], recvr.at[1 - side, k], hosts[1 + side]
            ).start()

    def turned(region, half):
        for k in (2 * half, 2 * half + 1):
            remote(
                rots.at[0, k], rots.at[region, k], sent.at[6], recvr.at[region - 1, k], peer
            ).wait_recv()

    def local_reply(region, half):
        return pltpu.make_async_copy(
            backs.at[half, FIRST[region] * 8 + seat],
            backr.at[half, hosts[region]],
            local.at[5 + 2 * region + half],
        )

    def rotate(region, half, away):
        g = FIRST[region] + away
        rows = pl.ds(pl.multiple_of(g * 8, 8), 8)
        x = gotm[rows].reshape(8 * 16, ORDER)
        r = jnp.concatenate([rots[region, 2 * half], rots[region, 2 * half + 1]], axis=1)
        y = jnp.dot(x, r, preferred_element_type=jnp.float32).astype(jnp.bfloat16)
        backs[half, rows] = y.reshape(8, 16, 2 * PANEL)
        place = line + (away if region == 1 else -away)

        def reply(k, _):
            t = share(k // 2, place, lax.rem(k, 2))
            ours = jnp.logical_or(away < 3, lax.rem(k, 2) == region - 1)

            @pl.when((t != me) & ours)
            def _():
                remote(
                    backs.at[half, g * 8 + k],
                    backr.at[half, hosts[region]],
                    sent.at[3 + region],
                    recvb,
                    t,
                ).start()

            return 0

        lax.fori_loop(0, 8, reply, 0)

    def rotate_half(half):
        @pl.when(active[0])
        def _():
            if half == 0:
                took(0, True)
            rotate(0, half, 0)
            local_reply(0, half).start()

        for region in (1, 2):

            @pl.when(active[region])
            def _():
                if half == 0:
                    took(region, True)
                turned(region, half)

        def pair(away, _):
            for region in (1, 2):

                @pl.when(active[region])
                def _():
                    rotate(region, half, away)

            return 0

        lax.fori_loop(0, 4, pair, 0)
        for region in (1, 2):

            @pl.when(active[region])
            def _():
                local_reply(region, half).start()

    def took(region, wait_in):
        count = 7 if region == 0 else 27
        if wait_in:
            part = gotm.at[0:count]
            remote(part, part, sent.at[2], recvm.at[region], peer).wait_recv()
        else:
            part = backs.at[:, 0:count]
            remote(part, part, sent.at[3 + region], recvb, peer).wait_send()

    def post_moments():
        lax.fori_loop(0, SHARES, postm, 0)
        for region in range(3):
            gotm[(0, 8, 40)[region] + seat] = sendm[hosts[region]]

    pl.semaphore_wait(barrier, SHARES - 1)
    post(0, pack0, send0, got0, recv0)
    post(1, pack1, send1, got1, recv1)
    fetches[3].wait()
    post_moments()

    def step(i, _):
        @pl.when(i == 0)
        def _():
            arrive(0, got0, recv0)
            load(0)

        @pl.when(i == 4)
        def _():
            keep(0)

            arrive(1, got1, recv1)
            load(1)

        for half in range(2):

            @pl.when(i == 6)
            def _():
                rotate_half(half)

        panel_step(lax.rem(i, 4))

        @pl.when((i < 4) & active[0])
        def _():
            turn(lax.rem(i, 4))

        return 0

    lax.fori_loop(0, 8, step, 0)
    keep(1)

    @pl.when(few)
    def _():
        part = backr.at[:, 0:53]
        remote(part, part, sent.at[2], recvb, peer).wait_recv()

    @pl.when(jnp.logical_not(few))
    def _():
        part = backr.at[:, 0:54]
        remote(part, part, sent.at[2], recvb, peer).wait_recv()

    flush(0, send0)
    flush(1, send1)

    @pl.when(few)
    def _():
        remote(sendm.at[0:53], sendm.at[0:53], sent.at[2], recvb, peer).wait_send()

    @pl.when(jnp.logical_not(few))
    def _():
        remote(sendm.at[0:54], sendm.at[0:54], sent.at[2], recvb, peer).wait_send()

    for region in range(3):

        @pl.when(active[region])
        def _():
            took(region, False)
            for half in range(2):
                local_reply(region, half).wait()

    @pl.when(active[0])
    def _():
        remote(rots.at[0:2], rots.at[0:2], sent.at[6], recvb, peer).wait_send()


def plan(owners, planned):
    shape = (PANEL, PANEL)
    sub = lax.broadcasted_iota(jnp.int32, shape, 0)
    lane = lax.broadcasted_iota(jnp.int32, shape, 1)
    row = jnp.broadcast_to(
        jnp.concatenate([owners[...], jnp.full((1, PANEL - BLOCKS), -1, jnp.int32)], axis=1), shape
    )
    column = row.T

    def across(x):
        return jnp.broadcast_to(jnp.sum(x.astype(jnp.int32), axis=1, keepdims=True), shape)

    def down(x):
        return jnp.broadcast_to(jnp.sum(x.astype(jnp.int32), axis=0, keepdims=True), shape)

    def resting(t):
        return ((t & 1) == 1) & (((t >> 1) & 3) == (t >> 4))

    same = column == row
    rank_c = across(same & (lane < sub))
    rank_r = down(same & (sub < lane))
    mine = column == lane
    first = mine & (rank_c == 0)
    second = mine & (rank_c == 1)
    owned_r = down(mine)
    owned_c = across(row == sub)
    vacant_r = (owned_r == 0) & jnp.logical_not(resting(lane)) & (lane < SHARES)
    vacant_c = (owned_c == 0) & jnp.logical_not(resting(sub)) & (sub < SHARES)
    guest_c = (column >= 0) & ((rank_c == 1) | resting(column))
    guest_r = (row >= 0) & ((rank_r == 1) | resting(row))
    vacant_at = down(vacant_c & (sub < lane))
    guest_at = across(guest_r & (lane < sub))
    hosted = guest_c & vacant_r & (vacant_at == guest_at)
    zero = jnp.zeros(shape, jnp.int32)
    moved = hosted | (first & jnp.logical_not(resting(lane)))
    rows = (
        down(jnp.where(first | hosted, sub, zero)),
        down(jnp.where(second, sub, zero)),
        across(jnp.where(moved, lane, zero)).T,
        owned_r,
        down(second),
    )
    planned[...] = jnp.zeros(planned.shape, jnp.int32)
    for i, x in enumerate(rows):
        planned[i:i + 1, :] = x[0:1, :]


def place_kernel(table, rows, bases, moment_out, owner_basis, sems):
    keeps = []
    for slot in range(SLOTS):
        keeps.append(
            pltpu.make_async_copy(bases.at[0, slot], owner_basis.at[0, slot], sems.at[1 + slot])
        )
        keeps[slot].start()

    def place(b, _):
        for half in range(2):
            pltpu.make_async_copy(
                rows.at[half, table[2, b]],
                moment_out.at[b, :, 2 * PANEL * half:2 * PANEL * (half + 1)],
                sems.at[0],
            ).start()
        return 0

    lax.fori_loop(0, BLOCKS, place, 0)
    pltpu.make_async_copy(moment_out, moment_out, sems.at[0]).wait()
    for keep in keeps:
        keep.wait()


def per_device(factor, old_basis, moment, owner_table):
    bf16 = jnp.bfloat16
    vmem = pl.BlockSpec(memory_space=pltpu.VMEM)
    hbm = pl.BlockSpec(memory_space=pl.ANY)
    kept = jax.ShapeDtypeStruct((1, SLOTS, ORDER, ORDER), bf16)
    table = owner_table.reshape(1, BLOCKS)
    held = [
        pltpu.with_memory_space_constraint(x, pltpu.HBM)
        for x in (table, factor, old_basis, moment)
    ]
    backs, bases, table = pl.pallas_call(
        refresh_kernel,
        out_shape=(
            jax.ShapeDtypeStruct((2, SHARES, 16, 2 * PANEL), bf16),
            kept,
            jax.ShapeDtypeStruct((8, PANEL), jnp.int32),
        ),
        in_specs=[hbm] * 4,
        out_specs=(vmem, vmem, vmem),
        scratch_shapes=[
            pltpu.VMEM((SHARES, 8, WIDTHS[0][0]), bf16),
            pltpu.VMEM((SHARES, 8, WIDTHS[1][0]), bf16),
            pltpu.VMEM((SHARES, 16, ORDER), bf16),
            pltpu.VMEM((SHARES, 8, WIDTHS[0][0]), bf16),
            pltpu.VMEM((SHARES, 8, WIDTHS[1][0]), bf16),
            pltpu.VMEM((72, 16, ORDER), bf16),
            pltpu.VMEM((2, 72, 16, 2 * PANEL), bf16),
            pltpu.VMEM((ORDER, ORDER), bf16),
            pltpu.VMEM((ORDER, 2 * ORDER), jnp.float32),
            pltpu.VMEM((PANEL, PANEL), jnp.float32),
            pltpu.VMEM((PANEL, PANEL), jnp.float32),
            pltpu.VMEM((3, 4, ORDER, PANEL), bf16),
            pltpu.VMEM(table.shape, jnp.int32),
            pltpu.VMEM(factor.shape, bf16),
            pltpu.VMEM(old_basis.shape, bf16),
            pltpu.VMEM(moment.shape, bf16),
            pltpu.SMEM((8, PANEL), jnp.int32),
            pltpu.SemaphoreType.DMA((7,)),
            pltpu.SemaphoreType.DMA((2,)),
            pltpu.SemaphoreType.DMA((2,)),
            pltpu.SemaphoreType.DMA((3,)),
            pltpu.SemaphoreType.DMA((2, 4)),
            pltpu.SemaphoreType.DMA,
            pltpu.SemaphoreType.DMA((12,)),
        ],
        compiler_params=pltpu.CompilerParams(
            collective_id=0, has_side_effects=True, vmem_limit_bytes=40 * 2**20
        ),
        cost_estimate=pl.CostEstimate(flops=8 * 10**9, bytes_accessed=4 * 2**20, transcendentals=0),
    )(*held)
    return pl.pallas_call(
        place_kernel,
        out_shape=(jax.ShapeDtypeStruct(moment.shape, bf16), kept),
        in_specs=[pl.BlockSpec(memory_space=pltpu.SMEM), vmem, vmem],
        out_specs=(hbm, hbm),
        scratch_shapes=[pltpu.SemaphoreType.DMA((1 + SLOTS,))],
        compiler_params=pltpu.CompilerParams(vmem_limit_bytes=16 * 2**20),
    )(table, backs, bases)


def solution(mesh):
    in_specs = (
        P("layer", ("fsdp", "own"), None),
        P("layer", ("fsdp", "own"), None),
        P("layer", ("fsdp", "own"), None),
        P("layer", None),
    )
    out_specs = (P("layer", ("fsdp", "own"), None), P("layer", ("fsdp", "own"), None, None))
    return jax.shard_map(
        per_device, mesh=mesh, in_specs=in_specs, out_specs=out_specs, check_vma=False
    )
```
